512 devices in a mesh: seq: 64 (over z, y), head: 8 (over x, core).
Axes of the slice: x: 4, y: 4, z: 16, core: 2. Of those that a mesh axis runs over, the one named last changes fastest.
Arguments:
- queries: bfloat16 [65536, 4096], P('seq', 'head'), may hold values from -120 to 120
- keys: bfloat16 [65536, 4096], P('seq', 'head'), may hold values from -6 to 6
- values: bfloat16 [65536, 4096], P('seq', 'head'), may hold values from -54 to 54
- head_temp: float32 [32], P('head'), may hold values from 0.5 to 3
- norm_gain: float32 [4096], P('head'), may hold values from 0.25 to 1.75
Outputs:
- normed: bfloat16 [65536, 4096], P('seq', 'head')
The draws below stay inside these ranges and needn't reach their ends.
All inputs are finite; a program needn't handle non-finite values.
Results may differ from the reference program's by a relative error of at most 0.0034.
Values may be sent and summed in bfloat16 or wider, within the bound.
No kernel may reach another device: no remote copies, remote signals or barrier semaphores. Data moves between devices by JAX's collectives and lax.ppermute only.
A program may use at most 128 MiB of HBM per device.

```python
import math
import jax
import jax.numpy as jnp
from jax import lax

HEADS = 32
HEAD_DIM = 128
BLK = 128
TOKENS = 65536


def unit_noise(key, shape):
    gaussian = jax.random.normal(jax.random.fold_in(key, 11), shape, jnp.float32)
    return gaussian


def sinusoids(key):
    columns = HEADS * HEAD_DIM
    periods = jnp.exp(jax.random.uniform(jax.random.fold_in(key, 1), (columns,), jnp.float32, math.log(256.0), math.log(float(TOKENS))))
    phases = jax.random.uniform(jax.random.fold_in(key, 2), (columns,), jnp.float32, -math.pi, math.pi)
    positions = jnp.arange(TOKENS).astype(jnp.float32)[:, None]
    return math.sqrt(2.0) * jnp.sin(2.0 * math.pi * positions / periods[None, :] + phases[None, :])


def group_offsets(key):
    per_group = unit_noise(key, (TOKENS // 64, HEADS * HEAD_DIM))
    return jnp.repeat(per_group, 64, axis=0)


def shared_parts(key):
    smooth = sinusoids(jax.random.fold_in(key, 900))
    key_rough = unit_noise(jax.random.fold_in(key, 901), (TOKENS, HEADS * HEAD_DIM))
    key_offset = group_offsets(jax.random.fold_in(key, 902))
    return (smooth, key_rough, key_offset)


def blend(rough_part, smooth, smooth_weight, offset):
    mixed = math.sqrt(1.0 - smooth_weight) * rough_part + math.sqrt(smooth_weight) * smooth + offset
    return jnp.clip(mixed, -6.0, 6.0)


def draw_keys(key, part):
    smooth, key_rough, key_offset = shared_parts(key)
    return blend(key_rough, smooth, 0.5, key_offset).astype(jnp.bfloat16)


def draw_queries(key, part):
    smooth, key_rough, key_offset = shared_parts(key)
    key = jax.random.fold_in(key, 5)
    own_rough = unit_noise(jax.random.fold_in(key, 1), (TOKENS, HEADS * HEAD_DIM))
    return blend(own_rough, smooth, 0.5, 0.0).astype(jnp.bfloat16)


def draw_values(key, part):
    key = jax.random.fold_in(key, 7)
    spread_log = math.log(3.0)
    smooth_weight = 0.5
    rough_part = unit_noise(jax.random.fold_in(key, 1), (TOKENS, HEADS * HEAD_DIM))
    smooth = sinusoids(jax.random.fold_in(key, 2))
    offset = group_offsets(jax.random.fold_in(key, 3))
    base_values = blend(rough_part, smooth, smooth_weight, offset)
    head_number = (jnp.arange(HEADS * HEAD_DIM) // HEAD_DIM).astype(jnp.float32)
    rising = jnp.exp(spread_log * head_number / float(HEADS - 1))
    return (base_values * rising[None, :]).astype(jnp.bfloat16)


def steps_of(own_key, extent, pieces, least, high):
    gain, own = 1.0, jax.random.fold_in(own_key, 6)
    for axis_at, blocks in pieces:
        heights = jnp.exp(jax.random.uniform(jax.random.fold_in(own, axis_at), (blocks,), jnp.float32, least / len(pieces), high / len(pieces)))
        gain = gain * jnp.repeat(heights, extent[axis_at] // blocks).reshape([-1 if axis == axis_at else 1 for axis in range(len(extent))])
    return gain


def setup_inputs(seed: int = 0) -> dict:
    streams_of = jax.random.split(jax.random.key(seed), 6)
    return {
        "queries": draw_queries(jax.random.fold_in(streams_of[5], 71), 0),
        "keys": draw_keys(jax.random.fold_in(streams_of[5], 71), 0),
        "values": draw_values(jax.random.fold_in(streams_of[5], 71), 0),
        "head_temp": jnp.clip(jnp.exp(math.log(3.0) - 1.7917595 * jax.random.uniform(streams_of[3], (HEADS,), jnp.float32) ** steps_of(streams_of[3], (HEADS,), ((0, 8),), -0.2, 0.2)), 0.5, 3.0),
        "norm_gain": jnp.clip(1.0 + 0.15 * jax.random.normal(streams_of[4], (HEADS * HEAD_DIM,), jnp.float32), 0.25, 1.75),
    }


EPS = 1e-06
LOG_FOUR = math.log(4.0)

def coarsen(stacked, factor):
    leading, entries, columns = stacked.shape
    grouped = stacked.reshape(leading, entries // factor, factor, columns).astype(jnp.float32)
    return lax.optimization_barrier(jnp.mean(grouped, axis=2)).astype(jnp.bfloat16)

def pad_entries(stacked):
    return jnp.pad(stacked, ((0, 0), (BLK, BLK), (0, 0)))

def level_scores(query_rows, extended, ext_start, first_row, span_tokens, group_size, level_index, score_scale, total_rows):
    rows_here = query_rows.shape[0]
    groups = max(1, rows_here // span_tokens)
    per_group = rows_here // groups
    block_first = first_row // span_tokens * span_tokens
    start_entry = (block_first - span_tokens - ext_start) // group_size
    window_piece = lax.dynamic_slice_in_dim(extended, start_entry, (groups + 2) * BLK, 1)
    block_parts = window_piece.reshape(2, groups + 2, BLK, extended.shape[2])
    windows = jnp.concatenate((block_parts[:, :-2], block_parts[:, 1:-1], block_parts[:, 2:]), axis=2)
    grouped = query_rows.reshape(groups, per_group, query_rows.shape[1])
    raw_scores = jnp.einsum('gqd,gkd->gqk', grouped.astype(jnp.float32), windows[0].astype(jnp.float32))
    entry_index = (block_first // span_tokens - 1) * BLK + BLK * jnp.arange(groups, dtype=jnp.int32)[:, None] + jnp.arange(3 * BLK, dtype=jnp.int32)[None, :]
    entry_token = (entry_index * group_size)[:, None, :]
    query_token = (first_row + jnp.arange(rows_here, dtype=jnp.int32)).reshape(groups, per_group, 1)
    usable = (entry_token >= 0) & (entry_token < total_rows)
    if level_index > 0:
        inner_span = span_tokens // 4
        inner_low = (query_token // inner_span - 1) * inner_span
        usable = usable & jnp.logical_not((entry_token >= inner_low) & (entry_token < inner_low + 3 * inner_span))
    scores = jnp.where(usable, raw_scores * score_scale + level_index * LOG_FOUR, -jnp.inf)
    return (scores, usable, windows[1])

def far_scores(query_rows, farthest, first_row, score_scale, total_rows):
    rows_here = query_rows.shape[0]
    raw_scores = jnp.dot(query_rows, farthest[0].T, preferred_element_type=jnp.float32)
    entry_token = (jnp.arange(farthest.shape[1], dtype=jnp.int32) * 64)[None, :]
    query_token = (first_row + jnp.arange(rows_here, dtype=jnp.int32))[:, None]
    outer_span = 16 * BLK
    outer_low = (query_token // outer_span - 1) * outer_span
    usable = jnp.logical_not((entry_token >= outer_low) & (entry_token < outer_low + 3 * outer_span))
    usable = usable & (entry_token < total_rows)
    scores = jnp.where(usable, raw_scores * score_scale + 3.0 * LOG_FOUR, -jnp.inf)
    return (scores[None], usable[None], farthest[1][None])

def attend(levels, rows_here):
    row_max = None
    for scores, usable, unused_values in levels:
        level_max = lax.optimization_barrier(jnp.max(scores, axis=-1)).reshape(rows_here)
        row_max = level_max if row_max is None else jnp.maximum(row_max, level_max)
    denominator = jnp.zeros((rows_here,), jnp.float32)
    numerator = None
    for scores, usable, entry_values in levels:
        groups, per_group, unused_dim = scores.shape
        shifted = row_max.reshape(groups, per_group, 1)
        weights = jnp.where(usable, jnp.exp(scores - shifted), 0.0)
        denominator = denominator + lax.optimization_barrier(jnp.sum(weights, axis=-1)).reshape(rows_here)
        weights_low = weights.astype(jnp.bfloat16)
        term = jnp.einsum('gqk,gkd->gqd', weights_low.astype(jnp.float32), entry_values.astype(jnp.float32))
        term = term.reshape(rows_here, entry_values.shape[2])
        numerator = term if numerator is None else numerator + term
    return numerator / denominator[:, None]

def reference(queries, keys, values, head_temp, norm_gain):
    stacked = jnp.stack((keys, values))
    coarse_one = coarsen(stacked, 4)
    coarse_two = coarsen(coarse_one, 4)
    coarse_three = coarsen(coarse_two, 4)

    def one_head(head_index):
        column = head_index * HEAD_DIM
        query_rows = lax.dynamic_slice_in_dim(queries, column, HEAD_DIM, 1)

        def select_head(array):
            return lax.dynamic_slice_in_dim(array, column, HEAD_DIM, 2)
        score_scale = head_temp[head_index] / math.sqrt(HEAD_DIM)
        levels = [level_scores(query_rows, pad_entries(select_head(stacked)), -BLK, 0, BLK, 1, 0, score_scale, TOKENS), level_scores(query_rows, pad_entries(select_head(coarse_one)), -4 * BLK, 0, 4 * BLK, 4, 1, score_scale, TOKENS), level_scores(query_rows, pad_entries(select_head(coarse_two)), -16 * BLK, 0, 16 * BLK, 16, 2, score_scale, TOKENS), far_scores(query_rows, select_head(coarse_three), 0, score_scale, TOKENS)]
        return attend(levels, TOKENS)
    per_head = lax.map(one_head, jnp.arange(HEADS, dtype=jnp.int32))
    attended = jnp.transpose(per_head, (1, 0, 2)).reshape(TOKENS, HEADS * HEAD_DIM)
    mean_square = lax.optimization_barrier(jnp.mean(attended * attended, axis=1))
    return (attended * lax.rsqrt(mean_square + EPS)[:, None] * norm_gain[None, :]).astype(jnp.bfloat16)
```

```python
import functools
import math

import jax
import jax.numpy as jnp
from jax import lax
from jax.experimental import pallas as pl
from jax.experimental.pallas import tpu as pltpu
from jax.sharding import PartitionSpec as P

HEADS = 32
HEAD_DIM = 128
BLK = 128
ROWS = 1024
HALF = 512
PAIR = 2 * HEAD_DIM
Y = 4
Z = 16

EPS = 1e-06
GONE = -1e30
NT = (((1,), (1,)), ((), ()))
BF = jnp.bfloat16
F32 = jnp.float32
VMEM_LIMIT = 48 * 1024 * 1024


def params():
    return pltpu.CompilerParams(vmem_limit_bytes=VMEM_LIMIT)


def cost(flops, moved, exps=0):
    return pl.CostEstimate(flops=flops, bytes_accessed=moved, transcendentals=exps)


def sds(shape, dtype):
    return jax.ShapeDtypeStruct(shape, dtype)


def prep_kernel(k_ref, v_ref, up_ref, down_ref, one_ref, two_ref, three_ref):
    rows = lax.broadcasted_iota(jnp.int32, (64, 256), 0)
    cols = lax.broadcasted_iota(jnp.int32, (64, 256), 1)
    pool = jnp.where(cols // 4 == rows, 0.25, 0.0).astype(BF)
    for which, ref in ((0, k_ref), (1, v_ref)):
        for pair in range(2):
            src = slice(pair * PAIR, (pair + 1) * PAIR)
            to = slice((2 * pair + which) * PAIR, (2 * pair + which + 1) * PAIR)
            for j in range(4):
                part = jnp.dot(pool, ref[256 * j : 256 * (j + 1), src], preferred_element_type=F32)
                one_ref[64 * j : 64 * (j + 1), to] = part.astype(BF)
            two = jnp.dot(pool, one_ref[:, to], preferred_element_type=F32).astype(BF)
            three = jnp.dot(pool[:16, :64], two, preferred_element_type=F32).astype(BF)
            two_ref[:, to] = two
            three_ref[:, to] = three
            up_ref[0:128, to] = ref[ROWS - 128 : ROWS, src]
            up_ref[128:256, to] = one_ref[128:256, to]
            down_ref[0:128, to] = ref[0:128, src]
            down_ref[128:256, to] = one_ref[0:128, to]


def prep(keys, values):
    return pl.pallas_call(
        prep_kernel,
        out_shape=(
            sds((256, 1024), BF),
            sds((256, 1024), BF),
            sds((256, 1024), BF),
            sds((64, 1024), BF),
            sds((16, 1024), BF),
        ),
        compiler_params=params(),
        cost_estimate=cost(700_000_000, 5_000_000),
    )(keys, values)


def near_kernel(
    pair, seq_size, dev_ref, temp_ref, q_ref, k_ref, v_ref,
    upk, upv, dnk, dnv, onk, onv, twok, twov, nextk, nextv,
    acc_ref, ml_ref,
):
    dev = dev_ref[0]
    c = temp_ref[2 * pair + pl.program_id(0)]
    z, y = dev // Y, dev % Y

    def gate(ok):
        return jnp.where(ok, 0.0, GONE).astype(F32)

    g_up = gate(dev >= 1)
    g_dn = gate(dev <= seq_size - 2)
    g_next = jnp.where(y < 2, gate(z >= 1), gate(z <= seq_size // Y - 2))

    lane384 = lax.broadcasted_iota(jnp.int32, (1, 384), 1)
    lane128 = lax.broadcasted_iota(jnp.int32, (128, 128), 1)
    k2 = jnp.concatenate([twok[...], nextk[...]], axis=0)
    v2 = jnp.concatenate([twov[...], nextv[...]], axis=0)
    next_first = jnp.where(y < 2, -2 * ROWS, 4 * ROWS) - 256 * 16
    token2 = lane384 * 16 - y * ROWS + jnp.where(lane384 < 256, 0, next_first)
    edge2 = jnp.where(lane384 < 256, 0.0, g_next)

    for g in range(2):
        base = g * HALF
        q = q_ref[base : base + HALF]
        if g == 0:
            k1 = jnp.concatenate([upk[128:256], onk[...]], axis=0)
            v1 = jnp.concatenate([upv[128:256], onv[...]], axis=0)
            edge1 = jnp.where(lane384 < 128, g_up, 0.0)
        else:
            k1 = jnp.concatenate([onk[...], dnk[128:256]], axis=0)
            v1 = jnp.concatenate([onv[...], dnv[128:256]], axis=0)
            edge1 = jnp.where(lane384 >= 256, g_dn, 0.0)
        inside = (token2 >= (g - 1) * HALF) & (token2 < (g + 2) * HALF)
        bias2 = jnp.where(inside, GONE, edge2)
        s1 = lax.dot_general(q, k1, NT, preferred_element_type=F32)
        s2 = lax.dot_general(q, k2, NT, preferred_element_type=F32)
        low1, low2, terms = [], [], []
        for b in range(4):
            block = 4 * g + b
            rows = slice(128 * b, 128 * (b + 1))
            if block == 0:
                k0 = jnp.concatenate([upk[0:128], k_ref[0:256]], axis=0)
                v0 = jnp.concatenate([upv[0:128], v_ref[0:256]], axis=0)
            elif block == 7:
                k0 = jnp.concatenate([k_ref[768:1024], dnk[0:128]], axis=0)
                v0 = jnp.concatenate([v_ref[768:1024], dnv[0:128]], axis=0)
            else:
                k0 = k_ref[128 * (block - 1) : 128 * (block + 2)]
                v0 = v_ref[128 * (block - 1) : 128 * (block + 2)]
            t0 = lax.dot_general(q[rows], k0, NT, preferred_element_type=F32)
            if block == 0:
                t0 = t0 + jnp.where(lane384 < 128, g_up, 0.0)
            if block == 7:
                t0 = t0 + jnp.where(lane384 >= 256, g_dn, 0.0)
            hidden = (lane384 >= 32 * b + 96) & (lane384 < 32 * b + 192)
            t1 = s1[rows] + jnp.where(hidden, GONE, edge1)
            t2 = s2[rows] + bias2
            top = jnp.maximum(
                c * jnp.max(t0, axis=1, keepdims=True),
                jnp.maximum(
                    c * jnp.max(t1, axis=1, keepdims=True) + 2.0,
                    c * jnp.max(t2, axis=1, keepdims=True) + 4.0,
                ),
            )
            w0 = jnp.exp2(c * t0 - top)
            w1 = jnp.exp2(c * t1 - (top - 2.0))
            w2 = jnp.exp2(c * t2 - (top - 4.0))
            total = (
                jnp.sum(w0, axis=1, keepdims=True)
                + jnp.sum(w1, axis=1, keepdims=True)
                + jnp.sum(w2, axis=1, keepdims=True)
            )
            low1.append(w1.astype(BF))
            low2.append(w2.astype(BF))
            terms.append(jnp.dot(w0.astype(BF), v0, preferred_element_type=F32))
            ml_ref[base + 128 * b : base + 128 * (b + 1)] = jnp.where(lane128 < 64, top, total)
        far = jnp.dot(jnp.concatenate(low1, axis=0), v1, preferred_element_type=F32)
        far = far + jnp.dot(jnp.concatenate(low2, axis=0), v2, preferred_element_type=F32)
        acc_ref[base : base + HALF] = jnp.concatenate(terms, axis=0) + far


def near(pair, seq_size, dev, temp, queries, keys, values, up, down, one, two, beyond):
    smem = pl.BlockSpec(memory_space=pltpu.SMEM)

    def own(rows):
        return pl.BlockSpec((rows, HEAD_DIM), lambda i: (0, 2 * pair + i))

    def packed(rows):
        return [
            pl.BlockSpec((rows, HEAD_DIM), lambda i: (0, 4 * pair + i)),
            pl.BlockSpec((rows, HEAD_DIM), lambda i: (0, 4 * pair + 2 + i)),
        ]

    out = pl.BlockSpec((ROWS, HEAD_DIM), lambda i: (0, i))
    return pl.pallas_call(
        functools.partial(near_kernel, pair, seq_size),
        grid=(2,),
        in_specs=[smem, smem, own(ROWS), own(ROWS), own(ROWS)]
        + packed(256) + packed(256) + packed(256) + packed(256) + packed(128),
        out_specs=(out, out),
        out_shape=(sds((ROWS, PAIR), F32), sds((ROWS, PAIR), F32)),
        compiler_params=params(),
        cost_estimate=cost(2_000_000_000, 6_000_000, 2_500_000),
    )(dev, temp, queries, keys, values, up, up, down, down, one, one, two, two, beyond, beyond)


CHUNK = 256


def far_kernel(pair, has_sum, dev_ref, temp_ref, q_ref, acc_ref, ml_ref, f0, f1, f2, f3, *rest):
    if has_sum:
        before_ref, att_ref, sum_ref = rest
    else:
        att_ref, sum_ref = rest
    dev = dev_ref[0]
    y, own_pair = dev % Y, dev // 2
    lane = lax.broadcasted_iota(jnp.int32, (1, 256), 1)
    blocks = (f0, f1, f2, f3)
    biases = []
    for k in range(4):
        src_pair = (lane // 16 * Y + (y + k) % Y) // 2
        seen = (src_pair < own_pair - 1) | (src_pair > own_pair + 1)
        biases.append(jnp.where(seen, 0.0, GONE).astype(F32))
    squares = None
    for i in range(2):
        c = temp_ref[2 * pair + i]
        cols = slice(HEAD_DIM * i, HEAD_DIM * (i + 1))
        vcols = slice(PAIR + HEAD_DIM * i, PAIR + HEAD_DIM * (i + 1))
        q = q_ref[:, cols]
        scores = [
            lax.dot_general(q, f[:, cols], NT, preferred_element_type=F32) + bias
            for f, bias in zip(blocks, biases)
        ]
        best = jnp.maximum(
            jnp.maximum(scores[0], scores[1]), jnp.maximum(scores[2], scores[3])
        )
        best = c * jnp.max(best, axis=1, keepdims=True) + 6.0
        top_near = ml_ref[:, HEAD_DIM * i : HEAD_DIM * i + 1]
        sum_near = ml_ref[:, HEAD_DIM * i + 64 : HEAD_DIM * i + 65]
        top = jnp.maximum(top_near, best)
        alpha = jnp.exp2(top_near - top)
        weights = [jnp.exp2(c * s - (top - 6.0)) for s in scores]
        total = alpha * sum_near + jnp.sum(
            (weights[0] + weights[1]) + (weights[2] + weights[3]), axis=1, keepdims=True
        )
        acc = acc_ref[:, cols] * alpha
        for w, f in zip(weights, blocks):
            acc = acc + jnp.dot(w.astype(BF), f[:, vcols], preferred_element_type=F32)
        att = acc / total
        att_ref[:, cols] = att
        squares = att * att if squares is None else squares + att * att
    for j in range(CHUNK // 128):
        rows = slice(128 * j, 128 * (j + 1))
        line = jnp.sum(jnp.transpose(squares[rows]), axis=0, keepdims=True)
        if has_sum:
            line = line + before_ref[:, rows]
        sum_ref[:, rows] = line


def far(pair, dev, temp, queries, acc, ml, columns, before):
    smem = pl.BlockSpec(memory_space=pltpu.SMEM)
    row = pl.BlockSpec((CHUNK, PAIR), lambda i: (i, 0))
    whole = pl.BlockSpec((256, 512), lambda i: (0, pair))
    part = pl.BlockSpec((256, 512), lambda i: (0, 0))
    line = pl.BlockSpec((1, CHUNK), lambda i: (0, i))
    extra = [] if before is None else [before]
    return pl.pallas_call(
        functools.partial(far_kernel, pair, before is not None),
        grid=(ROWS // CHUNK,),
        in_specs=[smem, smem, pl.BlockSpec((CHUNK, PAIR), lambda i: (i, pair)), row, row]
        + [whole, whole, part, whole] + [line] * len(extra),
        out_specs=(row, line),
        out_shape=(sds((ROWS, PAIR), F32), sds((1, ROWS), F32)),
        compiler_params=params(),
        cost_estimate=cost(1_200_000_000, 5_000_000, 2_100_000),
    )(dev, temp, queries, acc, ml, *columns, *extra)


def norm_kernel(a_ref, b_ref, sum_ref, gain_ref, out_ref):
    mean = jnp.sum(sum_ref[...], axis=0, keepdims=True) / (HEADS * HEAD_DIM)
    inverse = lax.rsqrt(mean + EPS)
    for j in range(CHUNK // 128):
        rows = slice(128 * j, 128 * (j + 1))
        tall = jnp.transpose(jnp.broadcast_to(inverse[:, rows], (128, 128)))
        for h in range(4):
            ref = a_ref if h < 2 else b_ref
            cols = slice(HEAD_DIM * (h % 2), HEAD_DIM * (h % 2 + 1))
            to = slice(HEAD_DIM * h, HEAD_DIM * (h + 1))
            out_ref[rows, to] = (ref[rows, cols] * tall * gain_ref[:, to]).astype(BF)


def norm(att_a, att_b, sums, gain):
    row = pl.BlockSpec((CHUNK, PAIR), lambda i: (i, 0))
    line = pl.BlockSpec((8, CHUNK), lambda i: (0, i))
    return pl.pallas_call(
        norm_kernel,
        grid=(ROWS // CHUNK,),
        in_specs=[row, row, line, pl.BlockSpec((1, 512), lambda i: (0, 0))],
        out_specs=pl.BlockSpec((CHUNK, 512), lambda i: (i, 0)),
        out_shape=sds((ROWS, 512), BF),
        compiler_params=params(),
        cost_estimate=cost(2_000_000, 3_000_000),
    )(att_a, att_b, sums, gain)


def fetch(value, axis, source):
    count = lax.axis_size(axis)
    return lax.ppermute(value, axis, [(source(i) % count, i) for i in range(count)])


def gathered(value, axis):
    size = lax.axis_size(axis)
    many = jnp.broadcast_to(value[None], (size,) + value.shape)
    return lax.all_to_all(many, axis, 0, 0, tiled=True)


Y_RING = [[z * Y + y for y in range(Y)] for z in range(Z)]
Z_RING = [[z * Y + y for z in range(Z)] for y in range(Y)]


def joined(value, groups):
    return lax.all_gather(value, "seq", axis_index_groups=groups, axis=0, tiled=True)


def local(queries, keys, values, head_temp, norm_gain):
    seq_size = lax.axis_size("seq")
    dev = lax.axis_index("seq").astype(jnp.int32).reshape(1)
    temp = head_temp * F32(math.log2(math.e) / math.sqrt(HEAD_DIM))
    up, down, one, two, three = prep(keys, values)

    from_up = fetch(up, "seq", lambda i: i - 1)
    from_down = fetch(down, "seq", lambda i: i + 1)
    group_two = joined(two, Y_RING)
    low_side = dev[0] % Y < 2
    other_half = jnp.where(low_side, group_two[128:], group_two[:128])
    beyond = fetch(other_half, "seq", lambda i: i - Y if i % Y < 2 else i + Y)

    column = joined(three, Z_RING)
    after = fetch(column, "seq", lambda i: i + 1)
    before = fetch(column, "seq", lambda i: i - 1)
    opposite_a = fetch(after[:, :512], "seq", lambda i: i + 1)
    opposite_b = fetch(before[:, 512:], "seq", lambda i: i - 1)

    near_args = (queries, keys, values, from_up, from_down, one, group_two, beyond)
    acc_a, ml_a = near(0, seq_size, dev, temp, *near_args)
    acc_b, ml_b = near(1, seq_size, dev, temp, *near_args)
    att_a, sum_a = far(0, dev, temp, queries, acc_a, ml_a, (column, after, opposite_a, before), None)
    att_b, sums = far(1, dev, temp, queries, acc_b, ml_b, (column, after, opposite_b, before), sum_a)
    sums = gathered(sums, "head").reshape(8, ROWS)
    return norm(att_a, att_b, sums, norm_gain.reshape(1, 512))


def solution(mesh):
    return jax.shard_map(
        local,
        mesh=mesh,
        in_specs=(P("seq", "head"), P("seq", "head"), P("seq", "head"), P("head"), P("head")),
        out_specs=P("seq", "head"),
        check_vma=False,
    )
```

```python
import functools
import math

import jax
import jax.numpy as jnp
from jax import lax
from jax.experimental import pallas as pl
from jax.experimental.pallas import tpu as pltpu
from jax.sharding import PartitionSpec as P

HEADS = 32
HEAD_DIM = 128
BLK = 128
ROWS = 1024
HALF = 512
PAIR = 2 * HEAD_DIM
Y = 4
Z = 16

EPS = 1e-06
GONE = -1e30
NT = (((1,), (1,)), ((), ()))
BF = jnp.bfloat16
F32 = jnp.float32
VMEM_LIMIT = 48 * 1024 * 1024


def params():
    return pltpu.CompilerParams(vmem_limit_bytes=VMEM_LIMIT)


def cost(flops, moved, exps=0):
    return pl.CostEstimate(flops=flops, bytes_accessed=moved, transcendentals=exps)


def sds(shape, dtype):
    return jax.ShapeDtypeStruct(shape, dtype)


def prep_kernel(k_ref, v_ref, up_ref, down_ref, one_ref, two_ref, three_ref):
    rows = lax.broadcasted_iota(jnp.int32, (64, 256), 0)
    cols = lax.broadcasted_iota(jnp.int32, (64, 256), 1)
    pool = jnp.where(cols // 4 == rows, 0.25, 0.0).astype(BF)
    for which, ref in ((0, k_ref), (1, v_ref)):
        for pair in range(2):
            src = slice(pair * PAIR, (pair + 1) * PAIR)
            to = slice((2 * pair + which) * PAIR, (2 * pair + which + 1) * PAIR)
            for j in range(4):
                part = jnp.dot(pool, ref[256 * j : 256 * (j + 1), src], preferred_element_type=F32)
                one_ref[64 * j : 64 * (j + 1), to] = part.astype(BF)
            two = jnp.dot(pool, one_ref[:, to], preferred_element_type=F32).astype(BF)
            three = jnp.dot(pool[:16, :64], two, preferred_element_type=F32).astype(BF)
            two_ref[:, to] = two
            three_ref[:, to] = three
            up_ref[0:128, to] = ref[ROWS - 128 : ROWS, src]
            up_ref[128:256, to] = one_ref[128:256, to]
            down_ref[0:128, to] = ref[0:128, src]
            down_ref[128:256, to] = one_ref[0:128, to]


def prep(keys, values):
    return pl.pallas_call(
        prep_kernel,
        out_shape=(
            sds((256, 1024), BF),
            sds((256, 1024), BF),
            sds((256, 1024), BF),
            sds((64, 1024), BF),
            sds((16, 1024), BF),
        ),
        compiler_params=params(),
        cost_estimate=cost(700_000_000, 5_000_000),
    )(keys, values)


def near_kernel(
    pair, seq_size, dev_ref, temp_ref, q_ref, k_ref, v_ref,
    upk, upv, dnk, dnv, onk, onv, twok, twov, nextk, nextv,
    acc_ref, ml_ref, sa, sb, pa, pb,
):
    dev = dev_ref[0]
    c = temp_ref[2 * pair + pl.program_id(0)]
    z, y = dev // Y, dev % Y

    def gate(ok):
        return jnp.where(ok, 0.0, GONE).astype(F32)

    g_up = gate(dev >= 1)
    g_dn = gate(dev <= seq_size - 2)
    g_next = jnp.where(y < 2, gate(z >= 1), gate(z <= seq_size // Y - 2))

    lane384 = lax.broadcasted_iota(jnp.int32, (1, 384), 1)
    lane128 = lax.broadcasted_iota(jnp.int32, (128, 128), 1)
    ones = jnp.ones((1152, 128), BF)
    next_first = jnp.where(y < 2, -2 * ROWS, 4 * ROWS) - 256 * 16
    token2 = lane384 * 16 - y * ROWS + jnp.where(lane384 < 256, 0, next_first)
    edge2 = jnp.where(lane384 < 256, 0.0, g_next)

    def window(b, own_ref, up_ref, dn_ref, one_ref, two_ref, next_ref):
        if b == 0:
            fine = [up_ref[0:128], own_ref[0:256]]
        elif b == 7:
            fine = [own_ref[768:1024], dn_ref[0:128]]
        else:
            fine = [own_ref[128 * (b - 1) : 128 * (b + 2)]]
        if b < 4:
            first = [up_ref[128:256], one_ref[...]]
        else:
            first = [one_ref[...], dn_ref[128:256]]
        return jnp.concatenate(fine + first + [two_ref[...], next_ref[...]], axis=0)

    def score(b):
        keys = window(b, k_ref, upk, dnk, onk, twok, nextk)
        scores = lax.dot_general(
            q_ref[128 * b : 128 * (b + 1)], keys, NT, preferred_element_type=F32
        )
        (sa, sb)[b % 2][...] = scores

    def bias_of(b):
        g = b // 4
        fine = None
        if b == 0:
            fine = jnp.where(lane384 < 128, g_up, 0.0)
        if b == 7:
            fine = jnp.where(lane384 >= 256, g_dn, 0.0)
        if g == 0:
            edge1 = jnp.where(lane384 < 128, g_up, 0.0)
        else:
            edge1 = jnp.where(lane384 >= 256, g_dn, 0.0)
        start = 32 * (b % 4) + 96
        hidden = (lane384 >= start) & (lane384 < start + 96)
        inside = (token2 >= (g - 1) * HALF) & (token2 < (g + 2) * HALF)
        first = jnp.where(hidden, GONE, edge1) + 2.0 / c
        second = jnp.where(inside, GONE, edge2) + 4.0 / c
        return fine, first, second

    score(0)
    for b in range(8):
        if b < 7:
            score(b + 1)
        s_ref, p_ref = (sa, sb)[b % 2], (pa, pb)[b % 2]
        fine, first, second = bias_of(b)
        for r in range(8):
            rows = slice(16 * r, 16 * (r + 1))
            parts = []
            for j in range(9):
                t = s_ref[rows, 128 * j : 128 * (j + 1)]
                bias = (fine, first, second)[j // 3]
                if bias is not None:
                    t = t + bias[:, 128 * (j % 3) : 128 * (j % 3 + 1)]
                parts.append(t)
            top = jnp.max(functools.reduce(jnp.maximum, parts), axis=1, keepdims=True)
            for j, t in enumerate(parts):
                p_ref[rows, 128 * j : 128 * (j + 1)] = jnp.exp2((t - top) * c).astype(BF)
            ml_ref[128 * b + 16 * r : 128 * b + 16 * (r + 1)] = jnp.broadcast_to(
                top * c, (16, 128)
            )
        vals = window(b, v_ref, upv, dnv, onv, twov, nextv)
        both = jnp.dot(
            p_ref[...], jnp.concatenate([vals, ones], axis=1), preferred_element_type=F32
        )
        rows = slice(128 * b, 128 * (b + 1))
        acc_ref[rows] = both[:, :128]
        ml_ref[rows] = jnp.where(lane128 < 64, ml_ref[rows], both[:, 128:])


def near(pair, seq_size, dev, temp, queries, keys, values, up, down, one, two, beyond):
    smem = pl.BlockSpec(memory_space=pltpu.SMEM)

    def own(rows):
        return pl.BlockSpec((rows, HEAD_DIM), lambda i: (0, 2 * pair + i))

    def packed(rows):
        return [
            pl.BlockSpec((rows, HEAD_DIM), lambda i: (0, 4 * pair + i)),
            pl.BlockSpec((rows, HEAD_DIM), lambda i: (0, 4 * pair + 2 + i)),
        ]

    out = pl.BlockSpec((ROWS, HEAD_DIM), lambda i: (0, i))
    return pl.pallas_call(
        functools.partial(near_kernel, pair, seq_size),
        grid=(2,),
        in_specs=[smem, smem, own(ROWS), own(ROWS), own(ROWS)]
        + packed(256) + packed(256) + packed(256) + packed(256) + packed(128),
        out_specs=(out, out),
        out_shape=(sds((ROWS, PAIR), F32), sds((ROWS, PAIR), F32)),
        scratch_shapes=[pltpu.VMEM((128, 1152), F32)] * 2 + [pltpu.VMEM((128, 1152), BF)] * 2,
        compiler_params=params(),
        cost_estimate=cost(2_000_000_000, 6_000_000, 2_500_000),
    )(dev, temp, queries, keys, values, up, up, down, down, one, one, two, two, beyond, beyond)


CHUNK = 256


def far_kernel(pair, has_sum, dev_ref, temp_ref, q_ref, acc_ref, ml_ref, f0, f1, f2, f3, *rest):
    if has_sum:
        before_ref, att_ref, sum_ref, sa, sb, pa, pb, a_ref = rest
    else:
        att_ref, sum_ref, sa, sb, pa, pb, a_ref = rest
    dev = dev_ref[0]
    y, own_pair = dev % Y, dev // 2
    lane = lax.broadcasted_iota(jnp.int32, (1, 256), 1)
    blocks = (f0, f1, f2, f3)
    biases = []
    for k in range(4):
        src_pair = (lane // 16 * Y + (y + k) % Y) // 2
        seen = (src_pair < own_pair - 1) | (src_pair > own_pair + 1)
        biases.append(jnp.where(seen, 0.0, GONE).astype(F32))
    bias = jnp.concatenate(biases, axis=1)
    ones = jnp.ones((1024, 128), BF)
    for i in range(2):
        cols = slice(HEAD_DIM * i, HEAD_DIM * (i + 1))
        keys = jnp.concatenate([f[:, cols] for f in blocks], axis=0)
        (sa, sb)[i][...] = lax.dot_general(
            q_ref[:, cols], keys, NT, preferred_element_type=F32
        )
    squares = None
    for i in range(2):
        c = temp_ref[2 * pair + i]
        cols = slice(HEAD_DIM * i, HEAD_DIM * (i + 1))
        vcols = slice(PAIR + HEAD_DIM * i, PAIR + HEAD_DIM * (i + 1))
        s_ref, p_ref = (sa, sb)[i], (pa, pb)[i]
        shifted = bias + 6.0 / c
        for r in range(CHUNK // 16):
            rows = slice(16 * r, 16 * (r + 1))
            parts = [
                s_ref[rows, 128 * j : 128 * (j + 1)] + shifted[:, 128 * j : 128 * (j + 1)]
                for j in range(8)
            ]
            best = jnp.max(functools.reduce(jnp.maximum, parts), axis=1, keepdims=True)
            top_near = ml_ref[rows, HEAD_DIM * i : HEAD_DIM * i + 1]
            top = jnp.maximum(top_near, c * best)
            for j, t in enumerate(parts):
                p_ref[rows, 128 * j : 128 * (j + 1)] = jnp.exp2(c * t - top).astype(BF)
            a_ref[rows] = jnp.broadcast_to(jnp.exp2(top_near - top), (16, 128))
        vals = jnp.concatenate([f[:, vcols] for f in blocks], axis=0)
        both = jnp.dot(
            p_ref[...], jnp.concatenate([vals, ones], axis=1), preferred_element_type=F32
        )
        alpha = a_ref[...]
        total = alpha * ml_ref[:, HEAD_DIM * i + 64 : HEAD_DIM * i + 65] + both[:, 128:]
        att = (acc_ref[:, cols] * alpha + both[:, :128]) / total
        att_ref[:, cols] = att
        squares = att * att if squares is None else squares + att * att
    for j in range(CHUNK // 128):
        rows = slice(128 * j, 128 * (j + 1))
        line = jnp.sum(jnp.transpose(squares[rows]), axis=0, keepdims=True)
        if has_sum:
            line = line + before_ref[:, rows]
        sum_ref[:, rows] = line


def far(pair, dev, temp, queries, acc, ml, columns, before):
    smem = pl.BlockSpec(memory_space=pltpu.SMEM)
    row = pl.BlockSpec((CHUNK, PAIR), lambda i: (i, 0))
    whole = pl.BlockSpec((256, 512), lambda i: (0, pair))
    part = pl.BlockSpec((256, 512), lambda i: (0, 0))
    line = pl.BlockSpec((1, CHUNK), lambda i: (0, i))
    extra = [] if before is None else [before]
    return pl.pallas_call(
        functools.partial(far_kernel, pair, before is not None),
        grid=(ROWS // CHUNK,),
        in_specs=[smem, smem, pl.BlockSpec((CHUNK, PAIR), lambda i: (i, pair)), row, row]
        + [whole, whole, part, whole] + [line] * len(extra),
        out_specs=(row, line),
        out_shape=(sds((ROWS, PAIR), F32), sds((1, ROWS), F32)),
        scratch_shapes=[pltpu.VMEM((CHUNK, 1024), F32)] * 2
        + [pltpu.VMEM((CHUNK, 1024), BF)] * 2
        + [pltpu.VMEM((CHUNK, 128), F32)],
        compiler_params=params(),
        cost_estimate=cost(1_200_000_000, 5_000_000, 2_100_000),
    )(dev, temp, queries, acc, ml, *columns, *extra)


def norm_kernel(a_ref, b_ref, sum_ref, gain_ref, out_ref):
    mean = jnp.sum(sum_ref[...], axis=0, keepdims=True) / (HEADS * HEAD_DIM)
    inverse = lax.rsqrt(mean + EPS)
    for j in range(CHUNK // 128):
        rows = slice(128 * j, 128 * (j + 1))
        tall = jnp.transpose(jnp.broadcast_to(inverse[:, rows], (128, 128)))
        for h in range(4):
            ref = a_ref if h < 2 else b_ref
            cols = slice(HEAD_DIM * (h % 2), HEAD_DIM * (h % 2 + 1))
            to = slice(HEAD_DIM * h, HEAD_DIM * (h + 1))
            out_ref[rows, to] = (ref[rows, cols] * tall * gain_ref[:, to]).astype(BF)


def norm(att_a, att_b, sums, gain):
    row = pl.BlockSpec((CHUNK, PAIR), lambda i: (i, 0))
    line = pl.BlockSpec((8, CHUNK), lambda i: (0, i))
    return pl.pallas_call(
        norm_kernel,
        grid=(ROWS // CHUNK,),
        in_specs=[row, row, line, pl.BlockSpec((1, 512), lambda i: (0, 0))],
        out_specs=pl.BlockSpec((CHUNK, 512), lambda i: (i, 0)),
        out_shape=sds((ROWS, 512), BF),
        compiler_params=params(),
        cost_estimate=cost(2_000_000, 3_000_000),
    )(att_a, att_b, sums, gain)


def fetch(value, axis, source):
    count = lax.axis_size(axis)
    return lax.ppermute(value, axis, [(source(i) % count, i) for i in range(count)])


def gathered(value, axis):
    size = lax.axis_size(axis)
    many = jnp.broadcast_to(value[None], (size,) + value.shape)
    return lax.all_to_all(many, axis, 0, 0, tiled=True)


Y_RING = [[z * Y + y for y in range(Y)] for z in range(Z)]
Z_RING = [[z * Y + y for z in range(Z)] for y in range(Y)]


def joined(value, groups):
    return lax.all_gather(value, "seq", axis_index_groups=groups, axis=0, tiled=True)


def local(queries, keys, values, head_temp, norm_gain):
    seq_size = lax.axis_size("seq")
    dev = lax.axis_index("seq").astype(jnp.int32).reshape(1)
    temp = head_temp * F32(math.log2(math.e) / math.sqrt(HEAD_DIM))
    up, down, one, two, three = prep(keys, values)

    from_up = fetch(up, "seq", lambda i: i - 1)
    from_down = fetch(down, "seq", lambda i: i + 1)
    group_two = joined(two, Y_RING)
    low_side = dev[0] % Y < 2
    other_half = jnp.where(low_side, group_two[128:], group_two[:128])
    beyond = fetch(other_half, "seq", lambda i: i - Y if i % Y < 2 else i + Y)

    three, beyond = lax.optimization_barrier((three, beyond))
    column = joined(three, Z_RING)
    after = fetch(column, "seq", lambda i: i + 1)
    before = fetch(column, "seq", lambda i: i - 1)
    opposite_a = fetch(after[:, :512], "seq", lambda i: i + 1)
    opposite_b = fetch(before[:, 512:], "seq", lambda i: i - 1)

    near_args = (queries, keys, values, from_up, from_down, one, group_two, beyond)
    acc_a, ml_a = near(0, seq_size, dev, temp, *near_args)
    acc_b, ml_b = near(1, seq_size, dev, temp, *near_args)
    att_a, sum_a = far(0, dev, temp, queries, acc_a, ml_a, (column, after, opposite_a, before), None)
    att_b, sums = far(1, dev, temp, queries, acc_b, ml_b, (column, after, opposite_b, before), sum_a)
    sums = gathered(sums, "head").reshape(8, ROWS)
    return norm(att_a, att_b, sums, norm_gain.reshape(1, 512))


def solution(mesh):
    return jax.shard_map(
        local,
        mesh=mesh,
        in_specs=(P("seq", "head"), P("seq", "head"), P("seq", "head"), P("head"), P("head")),
        out_specs=P("seq", "head"),
        check_vma=False,
    )
```

```python
import functools
import math

import jax
import jax.numpy as jnp
from jax import lax
from jax.experimental import pallas as pl
from jax.experimental.pallas import tpu as pltpu
from jax.sharding import PartitionSpec as P

HEADS = 32
HEAD_DIM = 128
BLK = 128
ROWS = 1024
HALF = 512
PAIR = 2 * HEAD_DIM
Y = 4
Z = 16

EPS = 1e-06
GONE = -1e30
NT = (((1,), (1,)), ((), ()))
BF = jnp.bfloat16
F32 = jnp.float32
VMEM_LIMIT = 48 * 1024 * 1024


def params():
    return pltpu.CompilerParams(vmem_limit_bytes=VMEM_LIMIT)


def cost(flops, moved, exps=0):
    return pl.CostEstimate(flops=flops, bytes_accessed=moved, transcendentals=exps)


def sds(shape, dtype):
    return jax.ShapeDtypeStruct(shape, dtype)


def prep_kernel(k_ref, v_ref, up_ref, down_ref, one_ref, two_ref, three_ref):
    rows = lax.broadcasted_iota(jnp.int32, (64, 256), 0)
    cols = lax.broadcasted_iota(jnp.int32, (64, 256), 1)
    pool = jnp.where(cols // 4 == rows, 0.25, 0.0).astype(BF)
    for which, ref in ((0, k_ref), (1, v_ref)):
        for pair in range(2):
            src = slice(pair * PAIR, (pair + 1) * PAIR)
            to = slice((2 * pair + which) * PAIR, (2 * pair + which + 1) * PAIR)
            for j in range(4):
                part = jnp.dot(pool, ref[256 * j : 256 * (j + 1), src], preferred_element_type=F32)
                one_ref[64 * j : 64 * (j + 1), to] = part.astype(BF)
            two = jnp.dot(pool, one_ref[:, to], preferred_element_type=F32).astype(BF)
            three = jnp.dot(pool[:16, :64], two, preferred_element_type=F32).astype(BF)
            two_ref[:, to] = two
            three_ref[:, to] = three
            up_ref[0:128, to] = ref[ROWS - 128 : ROWS, src]
            up_ref[128:256, to] = one_ref[128:256, to]
            down_ref[0:128, to] = ref[0:128, src]
            down_ref[128:256, to] = one_ref[0:128, to]


def prep(keys, values):
    return pl.pallas_call(
        prep_kernel,
        out_shape=(
            sds((256, 1024), BF),
            sds((256, 1024), BF),
            sds((256, 1024), BF),
            sds((64, 1024), BF),
            sds((16, 1024), BF),
        ),
        compiler_params=params(),
        cost_estimate=cost(700_000_000, 5_000_000),
    )(keys, values)


def near_kernel(
    pair, seq_size, dev_ref, temp_ref, q_all, k_all, v_all, up_all, down_all, one_all, two_all,
    next_all, acc_all, ml_all, sa, sb, pa, pb,
):
    def one_head(i, carry):
        near_head(
            pair, seq_size, i, dev_ref, temp_ref, q_all, k_all, v_all, up_all, down_all, one_all,
            two_all, next_all, acc_all, ml_all, sa, sb, pa, pb,
        )
        return carry

    lax.fori_loop(0, 2, one_head, 0)


def near_head(
    pair, seq_size, i, dev_ref, temp_ref, q_all, k_all, v_all, up_all, down_all, one_all, two_all,
    next_all, acc_all, ml_all, sa, sb, pa, pb,
):
    def head_cols(ref, first):
        return ref.at[:, pl.ds(pl.multiple_of(HEAD_DIM * (first + i), HEAD_DIM), HEAD_DIM)]

    q_ref, k_ref, v_ref = [head_cols(ref, 2 * pair) for ref in (q_all, k_all, v_all)]
    acc_ref, ml_ref = head_cols(acc_all, 0), head_cols(ml_all, 0)
    edges = (up_all, down_all, one_all, two_all, next_all)
    upk, dnk, onk, twok, nextk = [head_cols(ref, 4 * pair) for ref in edges]
    upv, dnv, onv, twov, nextv = [head_cols(ref, 4 * pair + 2) for ref in edges]
    dev = dev_ref[0]
    c = temp_ref[2 * pair + i]
    z, y = dev // Y, dev % Y

    def gate(ok):
        return jnp.where(ok, 0.0, GONE).astype(F32)

    g_up = gate(dev >= 1)
    g_dn = gate(dev <= seq_size - 2)
    g_next = jnp.where(y < 2, gate(z >= 1), gate(z <= seq_size // Y - 2))

    lane384 = lax.broadcasted_iota(jnp.int32, (1, 384), 1)
    lane128 = lax.broadcasted_iota(jnp.int32, (128, 128), 1)
    ones = jnp.ones((1152, 128), BF)
    next_first = jnp.where(y < 2, -2 * ROWS, 4 * ROWS) - 256 * 16
    token2 = lane384 * 16 - y * ROWS + jnp.where(lane384 < 256, 0, next_first)
    edge2 = jnp.where(lane384 < 256, 0.0, g_next)

    def window(b, own_ref, up_ref, dn_ref, one_ref, two_ref, next_ref):
        if b == 0:
            fine = [up_ref[0:128], own_ref[0:256]]
        elif b == 7:
            fine = [own_ref[768:1024], dn_ref[0:128]]
        else:
            fine = [own_ref[128 * (b - 1) : 128 * (b + 2)]]
        if b < 4:
            first = [up_ref[128:256], one_ref[...]]
        else:
            first = [one_ref[...], dn_ref[128:256]]
        return jnp.concatenate(fine + first + [two_ref[...], next_ref[...]], axis=0)

    def score(b):
        keys = window(b, k_ref, upk, dnk, onk, twok, nextk)
        scores = lax.dot_general(
            q_ref[128 * b : 128 * (b + 1)], keys, NT, preferred_element_type=F32
        )
        (sa, sb)[b % 2][...] = scores

    def bias_of(b):
        g = b // 4
        fine = None
        if b == 0:
            fine = jnp.where(lane384 < 128, g_up, 0.0)
        if b == 7:
            fine = jnp.where(lane384 >= 256, g_dn, 0.0)
        if g == 0:
            edge1 = jnp.where(lane384 < 128, g_up, 0.0)
        else:
            edge1 = jnp.where(lane384 >= 256, g_dn, 0.0)
        start = 32 * (b % 4) + 96
        hidden = (lane384 >= start) & (lane384 < start + 96)
        inside = (token2 >= (g - 1) * HALF) & (token2 < (g + 2) * HALF)
        first = jnp.where(hidden, GONE, edge1) + 2.0 / c
        second = jnp.where(inside, GONE, edge2) + 4.0 / c
        return fine, first, second

    score(0)
    for b in range(8):
        if b < 7:
            score(b + 1)
        s_ref, p_ref = (sa, sb)[b % 2], (pa, pb)[b % 2]
        fine, first, second = bias_of(b)
        for r in range(8):
            rows = slice(16 * r, 16 * (r + 1))
            parts = []
            for j in range(9):
                t = s_ref[rows, 128 * j : 128 * (j + 1)]
                bias = (fine, first, second)[j // 3]
                if bias is not None:
                    t = t + bias[:, 128 * (j % 3) : 128 * (j % 3 + 1)]
                parts.append(t)
            top = jnp.max(functools.reduce(jnp.maximum, parts), axis=1, keepdims=True)
            for j, t in enumerate(parts):
                p_ref[rows, 128 * j : 128 * (j + 1)] = jnp.exp2((t - top) * c).astype(BF)
            ml_ref[128 * b + 16 * r : 128 * b + 16 * (r + 1)] = jnp.broadcast_to(
                top * c, (16, 128)
            )
        vals = window(b, v_ref, upv, dnv, onv, twov, nextv)
        both = jnp.dot(
            p_ref[...], jnp.concatenate([vals, ones], axis=1), preferred_element_type=F32
        )
        rows = slice(128 * b, 128 * (b + 1))
        acc_ref[rows] = both[:, :128]
        ml_ref[rows] = jnp.where(lane128 < 64, ml_ref[rows], both[:, 128:])


def near(pair, seq_size, dev, temp, queries, keys, values, up, down, one, two, beyond):
    smem = pl.BlockSpec(memory_space=pltpu.SMEM)

    whole = pl.BlockSpec(memory_space=pltpu.VMEM)
    return pl.pallas_call(
        functools.partial(near_kernel, pair, seq_size),
        in_specs=[smem, smem] + [whole] * 8,
        out_specs=(whole, whole),
        out_shape=(sds((ROWS, PAIR), F32), sds((ROWS, PAIR), F32)),
        scratch_shapes=[pltpu.VMEM((128, 1152), F32)] * 2 + [pltpu.VMEM((128, 1152), BF)] * 2,
        compiler_params=params(),
        cost_estimate=cost(2_000_000_000, 6_000_000, 2_500_000),
    )(dev, temp, queries, keys, values, up, down, one, two, beyond)


CHUNK = 256


def far_kernel(
    pair, has_sum, dev_ref, temp_ref, q_ref, acc_ref, ml_ref, gain_ref, f0, f1, f2, f3, *rest
):
    if has_sum:
        before_ref, att_ref, sum_ref, sa, sb, pa, pb, a_ref = rest
    else:
        att_ref, sum_ref, sa, sb, pa, pb, a_ref = rest
    dev = dev_ref[0]
    y, own_pair = dev % Y, dev // 2
    lane = lax.broadcasted_iota(jnp.int32, (1, 256), 1)
    src_z = lane // 64 + 4 * (lane // 16 % 4)
    biases = []
    for k in range(4):
        src_pair = (src_z * Y + (y + k) % Y) // 2
        seen = (src_pair < own_pair - 1) | (src_pair > own_pair + 1)
        biases.append(jnp.where(seen, 0.0, GONE).astype(F32))
    bias = jnp.concatenate(biases, axis=1)
    ones = jnp.ones((1024, 128), BF)
    starts = [0 if f.shape[1] == 512 else 512 * pair for f in (f0, f1, f2, f3)]
    blocks = list(zip((f0, f1, f2, f3), starts))

    def column(which, i):
        return jnp.concatenate(
            [
                f[:, at + PAIR * which + HEAD_DIM * i : at + PAIR * which + HEAD_DIM * (i + 1)]
                for f, at in blocks
            ],
            axis=0,
        )

    def part(step, carry):
        first = step * HALF

        def place(unit):
            return pl.ds(pl.multiple_of(first + CHUNK * (unit // 2), CHUNK), CHUNK)

        def score(unit):
            i = unit % 2
            q = q_ref[place(unit), PAIR * pair + HEAD_DIM * i : PAIR * pair + HEAD_DIM * (i + 1)]
            (sa, sb)[i][...] = lax.dot_general(
                q, column(0, i), NT, preferred_element_type=F32
            )

        squares = None
        score(0)
        for unit in range(4):
            if unit < 3:
                score(unit + 1)
            i = unit % 2
            c = temp_ref[2 * pair + i]
            cols = slice(HEAD_DIM * i, HEAD_DIM * (i + 1))
            s_ref, p_ref = (sa, sb)[i], (pa, pb)[i]
            shifted = bias + 6.0 / c
            start = first + CHUNK * (unit // 2)
            for r in range(CHUNK // 16):
                rows = slice(16 * r, 16 * (r + 1))
                parts = [
                    s_ref[rows, 128 * j : 128 * (j + 1)] + shifted[:, 128 * j : 128 * (j + 1)]
                    for j in range(8)
                ]
                best = jnp.max(functools.reduce(jnp.maximum, parts), axis=1, keepdims=True)
                there = pl.ds(pl.multiple_of(start + 16 * r, 16), 16)
                top_near = ml_ref[there, HEAD_DIM * i : HEAD_DIM * i + 1]
                top = jnp.maximum(top_near, c * best)
                for j, t in enumerate(parts):
                    p_ref[rows, 128 * j : 128 * (j + 1)] = jnp.exp2(c * t - top).astype(BF)
                a_ref[rows] = jnp.broadcast_to(jnp.exp2(top_near - top), (16, 128))
            both = jnp.dot(
                p_ref[...],
                jnp.concatenate([column(1, i), ones], axis=1),
                preferred_element_type=F32,
            )
            alpha = a_ref[...]
            here = place(unit)
            total = alpha * ml_ref[here, HEAD_DIM * i + 64 : HEAD_DIM * i + 65] + both[:, 128:]
            att = (acc_ref[here, cols] * alpha + both[:, :128]) / total
            att_ref[here, cols] = att * gain_ref[:, PAIR * pair + HEAD_DIM * i : PAIR * pair + HEAD_DIM * (i + 1)]
            if i == 0:
                squares = att * att
                continue
            squares = squares + att * att
            for j in range(CHUNK // 128):
                line = jnp.sum(
                    jnp.transpose(squares[128 * j : 128 * (j + 1)]), axis=0, keepdims=True
                )
                lanes = pl.ds(pl.multiple_of(start + 128 * j, 128), 128)
                if has_sum:
                    line = line + before_ref[:, lanes]
                sum_ref[:, lanes] = line
        return carry

    lax.fori_loop(0, 2, part, 0)


def far(pair, dev, temp, queries, acc, ml, gain, columns, before):
    smem = pl.BlockSpec(memory_space=pltpu.SMEM)
    whole = pl.BlockSpec(memory_space=pltpu.VMEM)
    extra = [] if before is None else [before]
    return pl.pallas_call(
        functools.partial(far_kernel, pair, before is not None),
        in_specs=[smem, smem] + [whole] * (8 + len(extra)),
        out_specs=(whole, whole),
        out_shape=(sds((ROWS, PAIR), F32), sds((1, ROWS), F32)),
        scratch_shapes=[pltpu.VMEM((CHUNK, 1024), F32)] * 2
        + [pltpu.VMEM((CHUNK, 1024), BF)] * 2
        + [pltpu.VMEM((CHUNK, 128), F32)],
        compiler_params=params(),
        cost_estimate=cost(1_200_000_000, 5_000_000, 2_100_000),
    )(dev, temp, queries, acc, ml, gain, *columns, *extra)


def norm_kernel(a_ref, b_ref, sum_ref, out_ref):
    start = pl.program_id(0) * CHUNK
    for j in range(CHUNK // 128):
        rows = slice(128 * j, 128 * (j + 1))
        there = pl.ds(pl.multiple_of(start + 128 * j, 128), 128)
        mean = jnp.sum(sum_ref[:, there], axis=0, keepdims=True) / (HEADS * HEAD_DIM)
        inverse = lax.rsqrt(mean + EPS)
        tall = jnp.transpose(jnp.broadcast_to(inverse, (128, 128)))
        for h in range(4):
            ref = a_ref if h < 2 else b_ref
            cols = slice(HEAD_DIM * (h % 2), HEAD_DIM * (h % 2 + 1))
            to = slice(HEAD_DIM * h, HEAD_DIM * (h + 1))
            out_ref[rows, to] = (ref[there, cols] * tall).astype(BF)


def norm(att_a, att_b, sums):
    whole = pl.BlockSpec(memory_space=pltpu.VMEM)
    return pl.pallas_call(
        norm_kernel,
        grid=(ROWS // CHUNK,),
        in_specs=[whole, whole, whole],
        out_specs=pl.BlockSpec((CHUNK, 512), lambda i: (i, 0)),
        out_shape=sds((ROWS, 512), BF),
        compiler_params=params(),
        cost_estimate=cost(2_000_000, 3_000_000),
    )(att_a, att_b, sums)


def fetch(value, axis, source):
    count = lax.axis_size(axis)
    return lax.ppermute(value, axis, [(source(i) % count, i) for i in range(count)])


def gathered(value, axis):
    size = lax.axis_size(axis)
    many = jnp.broadcast_to(value[None], (size,) + value.shape)
    return lax.all_to_all(many, axis, 0, 0, tiled=True)


Y_RING = [[z * Y + y for y in range(Y)] for z in range(Z)]
Z_APART = [[(a + 4 * b) * Y + y for b in range(4)] for a in range(4) for y in range(Y)]
Z_NEXT = [[(a + 4 * b) * Y + y for a in range(4)] for b in range(4) for y in range(Y)]


def joined(value, groups):
    return lax.all_gather(value, "seq", axis_index_groups=groups, axis=0, tiled=True)


def local(queries, keys, values, head_temp, norm_gain):
    seq_size = lax.axis_size("seq")
    dev = lax.axis_index("seq").astype(jnp.int32).reshape(1)
    temp = head_temp * F32(math.log2(math.e) / math.sqrt(HEAD_DIM))
    up, down, one, two, three = prep(keys, values)

    from_up = fetch(up, "seq", lambda i: i - 1)
    from_down = fetch(down, "seq", lambda i: i + 1)
    group_two = joined(two, Y_RING)
    low_side = dev[0] % Y < 2
    other_half = jnp.where(low_side, group_two[128:], group_two[:128])
    beyond = fetch(other_half, "seq", lambda i: i - Y if i % Y < 2 else i + Y)

    three, beyond = lax.optimization_barrier((three, beyond))
    column = joined(three, Z_APART)
    column, from_up, from_down = lax.optimization_barrier((column, from_up, from_down))
    column = joined(column, Z_NEXT)
    after = fetch(column, "seq", lambda i: i + 1)
    before = fetch(column, "seq", lambda i: i - 1)
    opposite_a = fetch(after[:, :512], "seq", lambda i: i + 1)
    opposite_b = fetch(before[:, 512:], "seq", lambda i: i - 1)

    near_args = (queries, keys, values, from_up, from_down, one, group_two, beyond)
    acc_a, ml_a = near(0, seq_size, dev, temp, *near_args)
    acc_b, ml_b = near(1, seq_size, dev, temp, *near_args)
    gain = norm_gain.reshape(1, 512)
    att_a, sum_a = far(0, dev, temp, queries, acc_a, ml_a, gain, (column, after, opposite_a, before), None)
    att_b, sums = far(1, dev, temp, queries, acc_b, ml_b, gain, (column, after, opposite_b, before), sum_a)
    sums = gathered(sums, "head").reshape(8, ROWS)
    return norm(att_a, att_b, sums)


def solution(mesh):
    return jax.shard_map(
        local,
        mesh=mesh,
        in_specs=(P("seq", "head"), P("seq", "head"), P("seq", "head"), P("head"), P("head")),
        out_specs=P("seq", "head"),
        check_vma=False,
    )
```

```python
import functools
import math

import jax
import jax.numpy as jnp
from jax import lax
from jax.experimental import pallas as pl
from jax.experimental.pallas import tpu as pltpu
from jax.sharding import PartitionSpec as P

HEADS = 32
HEAD_DIM = 128
BLK = 128
ROWS = 1024
HALF = 512
PAIR = 2 * HEAD_DIM
Y = 4
Z = 16

EPS = 1e-06
GONE = -1e30
NT = (((1,), (1,)), ((), ()))
BF = jnp.bfloat16
F32 = jnp.float32
VMEM_LIMIT = 48 * 1024 * 1024


def params():
    return pltpu.CompilerParams(vmem_limit_bytes=VMEM_LIMIT)


def cost(flops, moved, exps=0):
    return pl.CostEstimate(flops=flops, bytes_accessed=moved, transcendentals=exps)


def sds(shape, dtype):
    return jax.ShapeDtypeStruct(shape, dtype)


def prep_kernel(k_ref, v_ref, up_ref, down_ref, one_ref, two_ref, three_ref):
    rows = lax.broadcasted_iota(jnp.int32, (64, 256), 0)
    cols = lax.broadcasted_iota(jnp.int32, (64, 256), 1)
    pool = jnp.where(cols // 4 == rows, 0.25, 0.0).astype(BF)
    for which, ref in ((0, k_ref), (1, v_ref)):
        for pair in range(2):
            src = slice(pair * PAIR, (pair + 1) * PAIR)
            to = slice((2 * pair + which) * PAIR, (2 * pair + which + 1) * PAIR)
            for j in range(4):
                part = jnp.dot(pool, ref[256 * j : 256 * (j + 1), src], preferred_element_type=F32)
                one_ref[64 * j : 64 * (j + 1), to] = part.astype(BF)
            two = jnp.dot(pool, one_ref[:, to], preferred_element_type=F32).astype(BF)
            three = jnp.dot(pool[:16, :64], two, preferred_element_type=F32).astype(BF)
            two_ref[:, to] = two
            three_ref[:, to] = three
            up_ref[0:128, to] = ref[ROWS - 128 : ROWS, src]
            up_ref[128:256, to] = one_ref[128:256, to]
            up_ref[256:320, to] = two
            down_ref[0:128, to] = ref[0:128, src]
            down_ref[128:256, to] = one_ref[0:128, to]
            down_ref[256:320, to] = two


def prep(keys, values):
    return pl.pallas_call(
        prep_kernel,
        out_shape=(
            sds((320, 1024), BF),
            sds((320, 1024), BF),
            sds((256, 1024), BF),
            sds((64, 1024), BF),
            sds((16, 1024), BF),
        ),
        compiler_params=params(),
        cost_estimate=cost(700_000_000, 5_000_000),
    )(keys, values)


def near_kernel(
    pair, seq_size, dev_ref, temp_ref, q_ref, k_ref, v_ref,
    upk, upv, dnk, dnv, onk, onv,
    acc_ref, ml_ref, sa, sb, pa, pb,
):
    dev = dev_ref[0]
    c = temp_ref[2 * pair + pl.program_id(0)]
    def gate(ok):
        return jnp.where(ok, 0.0, GONE).astype(F32)

    g_up = gate(dev >= 1)
    g_dn = gate(dev <= seq_size - 2)

    lane384 = lax.broadcasted_iota(jnp.int32, (1, 384), 1)
    lane128 = lax.broadcasted_iota(jnp.int32, (128, 128), 1)
    ones = jnp.ones((768, 128), BF)
    def window(b, own_ref, up_ref, dn_ref, one_ref):
        if b == 0:
            fine = [up_ref[0:128], own_ref[0:256]]
        elif b == 7:
            fine = [own_ref[768:1024], dn_ref[0:128]]
        else:
            fine = [own_ref[128 * (b - 1) : 128 * (b + 2)]]
        if b < 4:
            first = [up_ref[128:256], one_ref[...]]
        else:
            first = [one_ref[...], dn_ref[128:256]]
        return jnp.concatenate(fine + first, axis=0)

    def score(b):
        keys = window(b, k_ref, upk, dnk, onk)
        scores = lax.dot_general(
            q_ref[128 * b : 128 * (b + 1)], keys, NT, preferred_element_type=F32
        )
        (sa, sb)[b % 2][...] = scores

    def bias_of(b):
        g = b // 4
        fine = None
        if b == 0:
            fine = jnp.where(lane384 < 128, g_up, 0.0)
        if b == 7:
            fine = jnp.where(lane384 >= 256, g_dn, 0.0)
        if g == 0:
            edge1 = jnp.where(lane384 < 128, g_up, 0.0)
        else:
            edge1 = jnp.where(lane384 >= 256, g_dn, 0.0)
        start = 32 * (b % 4) + 96
        hidden = (lane384 >= start) & (lane384 < start + 96)
        return fine, jnp.where(hidden, GONE, edge1) + 2.0 / c

    score(0)
    for b in range(8):
        if b < 7:
            score(b + 1)
        s_ref, p_ref = (sa, sb)[b % 2], (pa, pb)[b % 2]
        fine, first = bias_of(b)
        for r in range(8):
            rows = slice(16 * r, 16 * (r + 1))
            parts = []
            for j in range(6):
                t = s_ref[rows, 128 * j : 128 * (j + 1)]
                bias = (fine, first)[j // 3]
                if bias is not None:
                    t = t + bias[:, 128 * (j % 3) : 128 * (j % 3 + 1)]
                parts.append(t)
            top = jnp.max(functools.reduce(jnp.maximum, parts), axis=1, keepdims=True)
            for j, t in enumerate(parts):
                p_ref[rows, 128 * j : 128 * (j + 1)] = jnp.exp2((t - top) * c).astype(BF)
            ml_ref[128 * b + 16 * r : 128 * b + 16 * (r + 1)] = jnp.broadcast_to(
                top * c, (16, 128)
            )
        vals = window(b, v_ref, upv, dnv, onv)
        both = jnp.dot(
            p_ref[...], jnp.concatenate([vals, ones], axis=1), preferred_element_type=F32
        )
        rows = slice(128 * b, 128 * (b + 1))
        acc_ref[rows] = both[:, :128]
        ml_ref[rows] = jnp.where(lane128 < 64, ml_ref[rows], both[:, 128:])


def near(pair, seq_size, dev, temp, queries, keys, values, up, down, one):
    smem = pl.BlockSpec(memory_space=pltpu.SMEM)

    def own(rows):
        return pl.BlockSpec((rows, HEAD_DIM), lambda i: (0, 2 * pair + i))

    def packed(rows):
        return [
            pl.BlockSpec((rows, HEAD_DIM), lambda i: (0, 4 * pair + i)),
            pl.BlockSpec((rows, HEAD_DIM), lambda i: (0, 4 * pair + 2 + i)),
        ]

    out = pl.BlockSpec((ROWS, HEAD_DIM), lambda i: (0, i))
    return pl.pallas_call(
        functools.partial(near_kernel, pair, seq_size),
        grid=(2,),
        in_specs=[smem, smem, own(ROWS), own(ROWS), own(ROWS)]
        + packed(320) + packed(320) + packed(256),
        out_specs=(out, out),
        out_shape=(sds((ROWS, PAIR), F32), sds((ROWS, PAIR), F32)),
        scratch_shapes=[pltpu.VMEM((128, 768), F32)] * 2 + [pltpu.VMEM((128, 768), BF)] * 2,
        compiler_params=params(),
        cost_estimate=cost(4_000_000_000, 6_000_000, 1_600_000),
    )(dev, temp, queries, keys, values, up, up, down, down, one, one)


CHUNK = 256


def far_kernel(
    pair, seq_size, has_sum, dev_ref, temp_ref, q_ref, acc_ref, ml_ref, gain_ref,
    two_ref, up_ref, down_ref, third_ref, own_ref, after_ref, before_ref, high_ref, low_ref, *rest
):
    if has_sum:
        partial_ref, att_ref, sum_ref, sa, sb, pa, pb, a_ref = rest
    else:
        att_ref, sum_ref, sa, sb, pa, pb, a_ref = rest
    dev = dev_ref[0]
    y, own_pair = dev % Y, dev // 2
    lane = lax.broadcasted_iota(jnp.int32, (1, 256), 1)
    order = lane // 16
    doubled = 8 * (order % 2) + 4 * (order // 2 % 2) + 2 * (order // 4 % 2) + order // 8
    far_bias = []
    for ahead in (0, 1, 2 - 4 * pair, -1):
        holder = (dev + ahead + seq_size) % seq_size
        src_pair = ((holder // Y + doubled) % Z * Y + holder % Y) // 2
        seen = (src_pair < own_pair - 1) | (src_pair > own_pair + 1)
        far_bias.append(jnp.where(seen, 0.0, GONE).astype(F32))
    lane64 = lax.broadcasted_iota(jnp.int32, (1, 64), 1)
    third = jnp.where(dev % 2 == 0, 3, -3)
    distances = (-2, -1, 0, 1, 2, third)
    base = 512 * pair
    width = 1408

    def column(which, i):
        offset = PAIR * which + HEAD_DIM * i
        wide = slice(base + offset, base + offset + HEAD_DIM)
        slim = slice(offset, offset + HEAD_DIM)
        relayed = slice(256 + 64 * pair, 320 + 64 * pair)
        opposite = (high_ref, low_ref)[pair]
        return jnp.concatenate(
            [
                own_ref[:, wide],
                after_ref[:, wide],
                opposite[0:256, slim],
                before_ref[:, wide],
                low_ref[relayed, slim],
                up_ref[256:320, wide],
                two_ref[:, wide],
                down_ref[256:320, wide],
                high_ref[relayed, slim],
                third_ref[:, wide],
            ],
            axis=0,
        )

    ones = jnp.ones((width, 128), BF)

    def part(step, carry):
        first = step * HALF

        def place(unit):
            return pl.ds(pl.multiple_of(first + CHUNK * (unit // 2), CHUNK), CHUNK)

        def score(unit):
            i = unit % 2
            q = q_ref[place(unit), PAIR * pair + HEAD_DIM * i : PAIR * pair + HEAD_DIM * (i + 1)]
            (sa, sb)[i][...] = lax.dot_general(
                q, column(0, i), NT, preferred_element_type=F32
            )

        two_bias = []
        for distance in distances:
            token = distance * ROWS + 16 * lane64
            source = dev + distance
            inside = (token >= (step - 1) * HALF) & (token < (step + 2) * HALF)
            there = (source >= 0) & (source < seq_size)
            two_bias.append(jnp.where(inside | jnp.logical_not(there), GONE, 0.0).astype(F32))
        two_bias = jnp.concatenate(two_bias, axis=1)
        squares = None
        score(0)
        for unit in range(4):
            if unit < 3:
                score(unit + 1)
            i = unit % 2
            c = temp_ref[2 * pair + i]
            cols = slice(HEAD_DIM * i, HEAD_DIM * (i + 1))
            s_ref, p_ref = (sa, sb)[i], (pa, pb)[i]
            shifted = jnp.concatenate(
                [b + 6.0 / c for b in far_bias] + [two_bias + 4.0 / c], axis=1
            )
            start = first + CHUNK * (unit // 2)
            for r in range(CHUNK // 16):
                rows = slice(16 * r, 16 * (r + 1))
                parts = [
                    s_ref[rows, 128 * j : 128 * (j + 1)] + shifted[:, 128 * j : 128 * (j + 1)]
                    for j in range(width // 128)
                ]
                best = jnp.max(functools.reduce(jnp.maximum, parts), axis=1, keepdims=True)
                there = pl.ds(pl.multiple_of(start + 16 * r, 16), 16)
                top_near = ml_ref[there, HEAD_DIM * i : HEAD_DIM * i + 1]
                top = jnp.maximum(top_near, c * best)
                for j, t in enumerate(parts):
                    p_ref[rows, 128 * j : 128 * (j + 1)] = jnp.exp2(c * t - top).astype(BF)
                a_ref[rows] = jnp.broadcast_to(jnp.exp2(top_near - top), (16, 128))
            both = jnp.dot(
                p_ref[...],
                jnp.concatenate([column(1, i), ones], axis=1),
                preferred_element_type=F32,
            )
            alpha = a_ref[...]
            here = place(unit)
            total = alpha * ml_ref[here, HEAD_DIM * i + 64 : HEAD_DIM * i + 65] + both[:, 128:]
            att = (acc_ref[here, cols] * alpha + both[:, :128]) / total
            att_ref[here, cols] = att * gain_ref[:, PAIR * pair + HEAD_DIM * i : PAIR * pair + HEAD_DIM * (i + 1)]
            if i == 0:
                squares = att * att
                continue
            squares = squares + att * att
            for j in range(CHUNK // 128):
                line = jnp.sum(
                    jnp.transpose(squares[128 * j : 128 * (j + 1)]), axis=0, keepdims=True
                )
                lanes = pl.ds(pl.multiple_of(start + 128 * j, 128), 128)
                if has_sum:
                    line = line + partial_ref[:, lanes]
                sum_ref[:, lanes] = line
        return carry

    lax.fori_loop(0, 2, part, 0)


def far(pair, seq_size, dev, temp, queries, acc, ml, gain, blocks, partial):
    smem = pl.BlockSpec(memory_space=pltpu.SMEM)
    whole = pl.BlockSpec(memory_space=pltpu.VMEM)
    extra = [] if partial is None else [partial]
    return pl.pallas_call(
        functools.partial(far_kernel, pair, seq_size, partial is not None),
        in_specs=[smem, smem] + [whole] * (4 + len(blocks) + len(extra)),
        out_specs=(whole, whole),
        out_shape=(sds((ROWS, PAIR), F32), sds((1, ROWS), F32)),
        scratch_shapes=[pltpu.VMEM((CHUNK, 1408), F32)] * 2
        + [pltpu.VMEM((CHUNK, 1408), BF)] * 2
        + [pltpu.VMEM((CHUNK, 128), F32)],
        compiler_params=params(),
        cost_estimate=cost(6_000_000_000, 5_000_000, 2_800_000),
    )(dev, temp, queries, acc, ml, gain, *blocks, *extra)


def norm_kernel(a_ref, b_ref, sum_ref, out_ref):
    start = pl.program_id(0) * CHUNK
    for j in range(CHUNK // 128):
        rows = slice(128 * j, 128 * (j + 1))
        there = pl.ds(pl.multiple_of(start + 128 * j, 128), 128)
        mean = jnp.sum(sum_ref[:, there], axis=0, keepdims=True) / (HEADS * HEAD_DIM)
        inverse = lax.rsqrt(mean + EPS)
        tall = jnp.transpose(jnp.broadcast_to(inverse, (128, 128)))
        for h in range(4):
            ref = a_ref if h < 2 else b_ref
            cols = slice(HEAD_DIM * (h % 2), HEAD_DIM * (h % 2 + 1))
            to = slice(HEAD_DIM * h, HEAD_DIM * (h + 1))
            out_ref[rows, to] = (ref[there, cols] * tall).astype(BF)


def norm(att_a, att_b, sums):
    whole = pl.BlockSpec(memory_space=pltpu.VMEM)
    return pl.pallas_call(
        norm_kernel,
        grid=(ROWS // CHUNK,),
        in_specs=[whole, whole, whole],
        out_specs=pl.BlockSpec((CHUNK, 512), lambda i: (i, 0)),
        out_shape=sds((ROWS, 512), BF),
        compiler_params=params(),
        cost_estimate=cost(2_000_000, 3_000_000),
    )(att_a, att_b, sums)


def fetch(value, axis, source):
    count = lax.axis_size(axis)
    return lax.ppermute(value, axis, [(source(i) % count, i) for i in range(count)])


def gathered(value, axis):
    size = lax.axis_size(axis)
    many = jnp.broadcast_to(value[None], (size,) + value.shape)
    return lax.all_to_all(many, axis, 0, 0, tiled=True)


def local(queries, keys, values, head_temp, norm_gain):
    seq_size = lax.axis_size("seq")
    dev = lax.axis_index("seq").astype(jnp.int32).reshape(1)
    temp = head_temp * F32(math.log2(math.e) / math.sqrt(HEAD_DIM))
    up, down, one, two, three = prep(keys, values)

    column = three
    for shift in (8, 4, 2, 1):
        column = jnp.concatenate([column, fetch(column, "seq", lambda i: i + Y * shift)], axis=0)
    from_up = fetch(up, "seq", lambda i: i - 1)
    from_down = fetch(down, "seq", lambda i: i + 1)
    third = fetch(two, "seq", lambda i: i + 3 if i % 2 == 0 else i - 3)
    after = fetch(column, "seq", lambda i: i + 1)
    before = fetch(column, "seq", lambda i: i - 1)

    def relay(half, edge):
        return jnp.concatenate([half, edge[256:, :512], edge[256:, 512:]], axis=0)

    high = fetch(relay(after[:, :512], from_down), "seq", lambda i: i + 1)
    low = fetch(relay(before[:, 512:], from_up), "seq", lambda i: i - 1)

    near_args = (queries, keys, values, from_up, from_down, one)
    acc_a, ml_a = near(0, seq_size, dev, temp, *near_args)
    acc_b, ml_b = near(1, seq_size, dev, temp, *near_args)
    gain = norm_gain.reshape(1, 512)
    blocks = (two, from_up, from_down, third, column, after, before, high, low)
    att_a, sum_a = far(0, seq_size, dev, temp, queries, acc_a, ml_a, gain, blocks, None)
    att_b, sums = far(1, seq_size, dev, temp, queries, acc_b, ml_b, gain, blocks, sum_a)
    sums = gathered(sums, "head").reshape(8, ROWS)
    return norm(att_a, att_b, sums)


def solution(mesh):
    return jax.shard_map(
        local,
        mesh=mesh,
        in_specs=(P("seq", "head"), P("seq", "head"), P("seq", "head"), P("head"), P("head")),
        out_specs=P("seq", "head"),
        check_vma=False,
    )
```

```python
import functools
import math

import jax
import jax.numpy as jnp
from jax import lax
from jax.experimental import pallas as pl
from jax.experimental.pallas import tpu as pltpu
from jax.sharding import PartitionSpec as P

HEADS = 32
HEAD_DIM = 128
BLK = 128
ROWS = 1024
HALF = 512
PAIR = 2 * HEAD_DIM
Y = 4
Z = 16

EPS = 1e-06
GONE = -1e30
NT = (((1,), (1,)), ((), ()))
BF = jnp.bfloat16
F32 = jnp.float32
VMEM_LIMIT = 20 * 1024 * 1024


def params():
    return pltpu.CompilerParams(vmem_limit_bytes=VMEM_LIMIT)


def cost(flops, moved, exps=0):
    return pl.CostEstimate(flops=flops, bytes_accessed=moved, transcendentals=exps)


def sds(shape, dtype):
    return jax.ShapeDtypeStruct(shape, dtype)


def prep_kernel(k_ref, v_ref, up_ref, down_ref, one_ref, two_ref, three_ref):
    rows = lax.broadcasted_iota(jnp.int32, (64, 256), 0)
    cols = lax.broadcasted_iota(jnp.int32, (64, 256), 1)
    pool = jnp.where(cols // 4 == rows, 0.25, 0.0).astype(BF)
    for which, ref in ((0, k_ref), (1, v_ref)):
        for pair in range(2):
            src = slice(pair * PAIR, (pair + 1) * PAIR)
            to = slice((2 * pair + which) * PAIR, (2 * pair + which + 1) * PAIR)
            for j in range(4):
                part = jnp.dot(pool, ref[256 * j : 256 * (j + 1), src], preferred_element_type=F32)
                one_ref[64 * j : 64 * (j + 1), to] = part.astype(BF)
            two = jnp.dot(pool, one_ref[:, to], preferred_element_type=F32).astype(BF)
            three = jnp.dot(pool[:16, :64], two, preferred_element_type=F32).astype(BF)
            two_ref[:, to] = two
            three_ref[:, to] = three
            up_ref[0:128, to] = ref[ROWS - 128 : ROWS, src]
            up_ref[128:256, to] = one_ref[128:256, to]
            up_ref[256:320, to] = two
            down_ref[0:128, to] = ref[0:128, src]
            down_ref[128:256, to] = one_ref[0:128, to]
            down_ref[256:320, to] = two


def prep(keys, values):
    return pl.pallas_call(
        prep_kernel,
        out_shape=(
            sds((320, 1024), BF),
            sds((320, 1024), BF),
            sds((256, 1024), BF),
            sds((64, 1024), BF),
            sds((16, 1024), BF),
        ),
        compiler_params=params(),
        cost_estimate=cost(700_000_000, 5_000_000),
    )(keys, values)


def near_kernel(
    pair, seq_size, dev_ref, temp_ref, q_ref, k_ref, v_ref,
    upk, upv, dnk, dnv, onk, onv,
    acc_ref, ml_ref, sa, sb, pa, pb,
):
    dev = dev_ref[0]
    c = temp_ref[2 * pair + pl.program_id(0)]
    def gate(ok):
        return jnp.where(ok, 0.0, GONE).astype(F32)

    g_up = gate(dev >= 1)
    g_dn = gate(dev <= seq_size - 2)

    lane384 = lax.broadcasted_iota(jnp.int32, (1, 384), 1)
    lane128 = lax.broadcasted_iota(jnp.int32, (128, 128), 1)
    ones = jnp.ones((768, 128), BF)
    def window(b, own_ref, up_ref, dn_ref, one_ref):
        if b == 0:
            fine = [up_ref[0:128], own_ref[0:256]]
        elif b == 7:
            fine = [own_ref[768:1024], dn_ref[0:128]]
        else:
            fine = [own_ref[128 * (b - 1) : 128 * (b + 2)]]
        if b < 4:
            first = [up_ref[128:256], one_ref[...]]
        else:
            first = [one_ref[...], dn_ref[128:256]]
        return jnp.concatenate(fine + first, axis=0)

    def score(b):
        keys = window(b, k_ref, upk, dnk, onk)
        scores = lax.dot_general(
            q_ref[128 * b : 128 * (b + 1)], keys, NT, preferred_element_type=F32
        )
        (sa, sb)[b % 2][...] = scores

    def bias_of(b):
        g = b // 4
        fine = None
        if b == 0:
            fine = jnp.where(lane384 < 128, g_up, 0.0)
        if b == 7:
            fine = jnp.where(lane384 >= 256, g_dn, 0.0)
        if g == 0:
            edge1 = jnp.where(lane384 < 128, g_up, 0.0)
        else:
            edge1 = jnp.where(lane384 >= 256, g_dn, 0.0)
        start = 32 * (b % 4) + 96
        hidden = (lane384 >= start) & (lane384 < start + 96)
        return fine, jnp.where(hidden, GONE, edge1) + 2.0 / c

    score(0)
    for b in range(8):
        if b < 7:
            score(b + 1)
        s_ref, p_ref = (sa, sb)[b % 2], (pa, pb)[b % 2]
        fine, first = bias_of(b)
        for r in range(8):
            rows = slice(16 * r, 16 * (r + 1))
            parts = []
            for j in range(6):
                t = s_ref[rows, 128 * j : 128 * (j + 1)]
                bias = (fine, first)[j // 3]
                if bias is not None:
                    t = t + bias[:, 128 * (j % 3) : 128 * (j % 3 + 1)]
                parts.append(t)
            top = jnp.max(functools.reduce(jnp.maximum, parts), axis=1, keepdims=True)
            for j, t in enumerate(parts):
                p_ref[rows, 128 * j : 128 * (j + 1)] = jnp.exp2((t - top) * c).astype(BF)
            ml_ref[128 * b + 16 * r : 128 * b + 16 * (r + 1)] = jnp.broadcast_to(
                top * c, (16, 128)
            )
        vals = window(b, v_ref, upv, dnv, onv)
        both = jnp.dot(
            p_ref[...], jnp.concatenate([vals, ones], axis=1), preferred_element_type=F32
        )
        rows = slice(128 * b, 128 * (b + 1))
        acc_ref[rows] = both[:, :128]
        ml_ref[rows] = jnp.where(lane128 < 64, ml_ref[rows], both[:, 128:])


def near(pair, seq_size, dev, temp, queries, keys, values, up, down, one):
    smem = pl.BlockSpec(memory_space=pltpu.SMEM)

    def own(rows):
        return pl.BlockSpec((rows, HEAD_DIM), lambda i: (0, 2 * pair + i))

    def packed(rows):
        return [
            pl.BlockSpec((rows, HEAD_DIM), lambda i: (0, 4 * pair + i)),
            pl.BlockSpec((rows, HEAD_DIM), lambda i: (0, 4 * pair + 2 + i)),
        ]

    out = pl.BlockSpec((ROWS, HEAD_DIM), lambda i: (0, i))
    return pl.pallas_call(
        functools.partial(near_kernel, pair, seq_size),
        grid=(2,),
        in_specs=[smem, smem, own(ROWS), own(ROWS), own(ROWS)]
        + packed(320) + packed(320) + packed(256),
        out_specs=(out, out),
        out_shape=(sds((ROWS, PAIR), F32), sds((ROWS, PAIR), F32)),
        scratch_shapes=[pltpu.VMEM((128, 768), F32)] * 2 + [pltpu.VMEM((128, 768), BF)] * 2,
        compiler_params=params(),
        cost_estimate=cost(4_000_000_000, 6_000_000, 1_600_000),
    )(dev, temp, queries, keys, values, up, up, down, down, one, one)


CHUNK = 256


def far_kernel(
    pair, seq_size, has_sum, dev_ref, temp_ref, q_ref, acc_ref, ml_ref, gain_ref,
    two_ref, up_ref, down_ref, third_ref, own_ref, after_ref, before_ref, high_ref, low_ref, *rest
):
    if has_sum:
        partial_ref, att_ref, sum_ref, sa, sb, pa, pb, a_ref = rest
    else:
        att_ref, sum_ref, sa, sb, pa, pb, a_ref = rest
    dev = dev_ref[0]
    y, own_pair = dev % Y, dev // 2
    lane = lax.broadcasted_iota(jnp.int32, (1, 256), 1)
    outer, inner = lane // 64, lane // 16 % 4
    away = jnp.where(outer == 3, -1, outer) + 4 * inner + Z
    far_bias = []
    for ahead in (0, 1, 2 - 4 * pair, -1):
        holder = (dev + ahead + seq_size) % seq_size
        src_pair = ((holder // Y + away) % Z * Y + holder % Y) // 2
        seen = (src_pair < own_pair - 1) | (src_pair > own_pair + 1)
        far_bias.append(jnp.where(seen, 0.0, GONE).astype(F32))
    lane64 = lax.broadcasted_iota(jnp.int32, (1, 64), 1)
    third = jnp.where(dev % 2 == 0, 3, -3)
    distances = (-2, -1, 0, 1, 2, third)
    base = 512 * pair
    width = 1408

    def column(which, i):
        offset = PAIR * which + HEAD_DIM * i
        wide = slice(base + offset, base + offset + HEAD_DIM)
        slim = slice(offset, offset + HEAD_DIM)
        relayed = slice(256 + 64 * pair, 320 + 64 * pair)
        opposite = (high_ref, low_ref)[pair]
        return jnp.concatenate(
            [
                own_ref[:, wide],
                after_ref[:, wide],
                opposite[0:256, slim],
                before_ref[:, wide],
                low_ref[relayed, slim],
                up_ref[256:320, wide],
                two_ref[:, wide],
                down_ref[256:320, wide],
                high_ref[relayed, slim],
                third_ref[:, wide],
            ],
            axis=0,
        )

    ones = jnp.ones((width, 128), BF)

    def part(step, carry):
        first = step * HALF

        def place(unit):
            return pl.ds(pl.multiple_of(first + CHUNK * (unit // 2), CHUNK), CHUNK)

        def score(unit):
            i = unit % 2
            q = q_ref[place(unit), PAIR * pair + HEAD_DIM * i : PAIR * pair + HEAD_DIM * (i + 1)]
            (sa, sb)[i][...] = lax.dot_general(
                q, column(0, i), NT, preferred_element_type=F32
            )

        two_bias = []
        for distance in distances:
            token = distance * ROWS + 16 * lane64
            source = dev + distance
            inside = (token >= (step - 1) * HALF) & (token < (step + 2) * HALF)
            there = (source >= 0) & (source < seq_size)
            two_bias.append(jnp.where(inside | jnp.logical_not(there), GONE, 0.0).astype(F32))
        two_bias = jnp.concatenate(two_bias, axis=1)
        squares = None
        score(0)
        for unit in range(4):
            if unit < 3:
                score(unit + 1)
            i = unit % 2
            c = temp_ref[2 * pair + i]
            cols = slice(HEAD_DIM * i, HEAD_DIM * (i + 1))
            s_ref, p_ref = (sa, sb)[i], (pa, pb)[i]
            shifted = jnp.concatenate(
                [b + 6.0 / c for b in far_bias] + [two_bias + 4.0 / c], axis=1
            )
            start = first + CHUNK * (unit // 2)
            for r in range(CHUNK // 16):
                rows = slice(16 * r, 16 * (r + 1))
                parts = [
                    s_ref[rows, 128 * j : 128 * (j + 1)] + shifted[:, 128 * j : 128 * (j + 1)]
                    for j in range(width // 128)
                ]
                best = jnp.max(functools.reduce(jnp.maximum, parts), axis=1, keepdims=True)
                there = pl.ds(pl.multiple_of(start + 16 * r, 16), 16)
                top_near = ml_ref[there, HEAD_DIM * i : HEAD_DIM * i + 1]
                top = jnp.maximum(top_near, c * best)
                for j, t in enumerate(parts):
                    p_ref[rows, 128 * j : 128 * (j + 1)] = jnp.exp2(c * t - top).astype(BF)
                a_ref[rows] = jnp.broadcast_to(jnp.exp2(top_near - top), (16, 128))
            both = jnp.dot(
                p_ref[...],
                jnp.concatenate([column(1, i), ones], axis=1),
                preferred_element_type=F32,
            )
            alpha = a_ref[...]
            here = place(unit)
            total = alpha * ml_ref[here, HEAD_DIM * i + 64 : HEAD_DIM * i + 65] + both[:, 128:]
            att = (acc_ref[here, cols] * alpha + both[:, :128]) / total
            att_ref[here, cols] = att * gain_ref[:, PAIR * pair + HEAD_DIM * i : PAIR * pair + HEAD_DIM * (i + 1)]
            if i == 0:
                squares = att * att
                continue
            squares = squares + att * att
            for j in range(CHUNK // 128):
                line = jnp.sum(
                    jnp.transpose(squares[128 * j : 128 * (j + 1)]), axis=0, keepdims=True
                )
                lanes = pl.ds(pl.multiple_of(start + 128 * j, 128), 128)
                if has_sum:
                    line = line + partial_ref[:, lanes]
                sum_ref[:, lanes] = line
        return carry

    lax.fori_loop(0, 2, part, 0)


def far(pair, seq_size, dev, temp, queries, acc, ml, gain, blocks, partial):
    smem = pl.BlockSpec(memory_space=pltpu.SMEM)
    whole = pl.BlockSpec(memory_space=pltpu.VMEM)
    extra = [] if partial is None else [partial]
    return pl.pallas_call(
        functools.partial(far_kernel, pair, seq_size, partial is not None),
        in_specs=[smem, smem] + [whole] * (4 + len(blocks) + len(extra)),
        out_specs=(whole, whole),
        out_shape=(sds((ROWS, PAIR), F32), sds((1, ROWS), F32)),
        scratch_shapes=[pltpu.VMEM((CHUNK, 1408), F32)] * 2
        + [pltpu.VMEM((CHUNK, 1408), BF)] * 2
        + [pltpu.VMEM((CHUNK, 128), F32)],
        compiler_params=params(),
        cost_estimate=cost(6_000_000_000, 5_000_000, 2_800_000),
    )(dev, temp, queries, acc, ml, gain, *blocks, *extra)


def norm_kernel(a_ref, b_ref, sum_ref, out_ref):
    start = pl.program_id(0) * CHUNK
    for j in range(CHUNK // 128):
        rows = slice(128 * j, 128 * (j + 1))
        there = pl.ds(pl.multiple_of(start + 128 * j, 128), 128)
        mean = jnp.sum(sum_ref[:, there], axis=0, keepdims=True) / (HEADS * HEAD_DIM)
        inverse = lax.rsqrt(mean + EPS)
        tall = jnp.transpose(jnp.broadcast_to(inverse, (128, 128)))
        for h in range(4):
            ref = a_ref if h < 2 else b_ref
            cols = slice(HEAD_DIM * (h % 2), HEAD_DIM * (h % 2 + 1))
            to = slice(HEAD_DIM * h, HEAD_DIM * (h + 1))
            out_ref[rows, to] = (ref[there, cols] * tall).astype(BF)


def norm(att_a, att_b, sums):
    whole = pl.BlockSpec(memory_space=pltpu.VMEM)
    return pl.pallas_call(
        norm_kernel,
        grid=(ROWS // CHUNK,),
        in_specs=[whole, whole, whole],
        out_specs=pl.BlockSpec((CHUNK, 512), lambda i: (i, 0)),
        out_shape=sds((ROWS, 512), BF),
        compiler_params=params(),
        cost_estimate=cost(2_000_000, 3_000_000),
    )(att_a, att_b, sums)


def fetch(value, axis, source):
    count = lax.axis_size(axis)
    return lax.ppermute(value, axis, [(source(i) % count, i) for i in range(count)])


def gathered(value, axis):
    size = lax.axis_size(axis)
    many = jnp.broadcast_to(value[None], (size,) + value.shape)
    return lax.all_to_all(many, axis, 0, 0, tiled=True)


def local(queries, keys, values, head_temp, norm_gain):
    seq_size = lax.axis_size("seq")
    dev = lax.axis_index("seq").astype(jnp.int32).reshape(1)
    temp = head_temp * F32(math.log2(math.e) / math.sqrt(HEAD_DIM))
    up, down, one, two, three = prep(keys, values)

    column = three
    for shifts in ((4, 8, -4), (1, 2, -1)):
        parts = [fetch(column, "seq", lambda i, s=s: i + Y * s) for s in shifts]
        column = jnp.concatenate([column] + parts, axis=0)
    from_up = fetch(up, "seq", lambda i: i - 1)
    from_down = fetch(down, "seq", lambda i: i + 1)
    third = fetch(two, "seq", lambda i: i + 3 if i % 2 == 0 else i - 3)
    near_args = (queries, keys, values, from_up, from_down, one)
    acc_a, ml_a = near(0, seq_size, dev, temp, *near_args)
    acc_b, ml_b = near(1, seq_size, dev, temp, *near_args)

    column, third, acc_a, ml_a = lax.optimization_barrier((column, third, acc_a, ml_a))
    after = fetch(column, "seq", lambda i: i + 1)
    before = fetch(column, "seq", lambda i: i - 1)

    def relay(half, edge):
        return jnp.concatenate([half, edge[256:, :512], edge[256:, 512:]], axis=0)

    high = relay(after[:, :512], from_down)
    low = relay(before[:, 512:], from_up)
    high, low, acc_b, ml_b = lax.optimization_barrier((high, low, acc_b, ml_b))
    high = fetch(high, "seq", lambda i: i + 1)
    low = fetch(low, "seq", lambda i: i - 1)

    gain = norm_gain.reshape(1, 512)
    blocks = (two, from_up, from_down, third, column, after, before, high, low)
    att_a, sum_a = far(0, seq_size, dev, temp, queries, acc_a, ml_a, gain, blocks, None)
    att_b, sums = far(1, seq_size, dev, temp, queries, acc_b, ml_b, gain, blocks, sum_a)
    sums = gathered(sums, "head").reshape(8, ROWS)
    return norm(att_a, att_b, sums)


def solution(mesh):
    return jax.shard_map(
        local,
        mesh=mesh,
        in_specs=(P("seq", "head"), P("seq", "head"), P("seq", "head"), P("head"), P("head")),
        out_specs=P("seq", "head"),
        check_vma=False,
    )
```

```python
import functools
import math

import jax
import jax.numpy as jnp
from jax import lax
from jax.experimental import pallas as pl
from jax.experimental.pallas import tpu as pltpu
from jax.sharding import PartitionSpec as P

HEADS = 32
HEAD_DIM = 128
BLK = 128
ROWS = 1024
HALF = 512
PAIR = 2 * HEAD_DIM
Y = 4
Z = 16

EPS = 1e-06
GONE = -1e30
NT = (((1,), (1,)), ((), ()))
BF = jnp.bfloat16
F32 = jnp.float32
VMEM_LIMIT = 48 * 1024 * 1024


def params():
    return pltpu.CompilerParams(vmem_limit_bytes=VMEM_LIMIT)


def cost(flops, moved, exps=0):
    return pl.CostEstimate(flops=flops, bytes_accessed=moved, transcendentals=exps)


def sds(shape, dtype):
    return jax.ShapeDtypeStruct(shape, dtype)


def prep_kernel(k_ref, v_ref, up_ref, down_ref, one_ref, two_ref, three_ref):
    rows = lax.broadcasted_iota(jnp.int32, (64, 256), 0)
    cols = lax.broadcasted_iota(jnp.int32, (64, 256), 1)
    pool = jnp.where(cols // 4 == rows, 0.25, 0.0).astype(BF)
    for which, ref in ((0, k_ref), (1, v_ref)):
        for pair in range(2):
            src = slice(pair * PAIR, (pair + 1) * PAIR)
            to = slice((2 * pair + which) * PAIR, (2 * pair + which + 1) * PAIR)
            for j in range(4):
                part = jnp.dot(pool, ref[256 * j : 256 * (j + 1), src], preferred_element_type=F32)
                one_ref[64 * j : 64 * (j + 1), to] = part.astype(BF)
            two = jnp.dot(pool, one_ref[:, to], preferred_element_type=F32).astype(BF)
            three = jnp.dot(pool[:16, :64], two, preferred_element_type=F32).astype(BF)
            two_ref[:, to] = two
            three_ref[:, to] = three
            up_ref[0:128, to] = ref[ROWS - 128 : ROWS, src]
            up_ref[128:256, to] = one_ref[128:256, to]
            down_ref[0:128, to] = ref[0:128, src]
            down_ref[128:256, to] = one_ref[0:128, to]


def prep(keys, values):
    return pl.pallas_call(
        prep_kernel,
        out_shape=(
            sds((256, 1024), BF),
            sds((256, 1024), BF),
            sds((256, 1024), BF),
            sds((64, 1024), BF),
            sds((16, 1024), BF),
        ),
        compiler_params=params(),
        cost_estimate=cost(700_000_000, 5_000_000),
    )(keys, values)


def near_kernel(
    pair, seq_size, dev_ref, temp_ref, q_ref, k_ref, v_ref,
    upk, upv, dnk, dnv, onk, onv, twok, twov, nextk, nextv,
    acc_ref, ml_ref, sa, sb, pa, pb,
):
    dev = dev_ref[0]
    c = temp_ref[2 * pair + pl.program_id(0)]
    z, y = dev // Y, dev % Y

    def gate(ok):
        return jnp.where(ok, 0.0, GONE).astype(F32)

    g_up = gate(dev >= 1)
    g_dn = gate(dev <= seq_size - 2)
    g_next = jnp.where(y < 2, gate(z >= 1), gate(z <= seq_size // Y - 2))

    lane384 = lax.broadcasted_iota(jnp.int32, (1, 384), 1)
    lane128 = lax.broadcasted_iota(jnp.int32, (128, 128), 1)
    ones = jnp.ones((1152, 128), BF)
    next_first = jnp.where(y < 2, -2 * ROWS, 4 * ROWS) - 256 * 16
    token2 = lane384 * 16 - y * ROWS + jnp.where(lane384 < 256, 0, next_first)
    edge2 = jnp.where(lane384 < 256, 0.0, g_next)

    def window(b, own_ref, up_ref, dn_ref, one_ref, two_ref, next_ref):
        if b == 0:
            fine = [up_ref[0:128], own_ref[0:256]]
        elif b == 7:
            fine = [own_ref[768:1024], dn_ref[0:128]]
        else:
            fine = [own_ref[128 * (b - 1) : 128 * (b + 2)]]
        if b < 4:
            first = [up_ref[128:256], one_ref[...]]
        else:
            first = [one_ref[...], dn_ref[128:256]]
        return jnp.concatenate(fine + first + [two_ref[...], next_ref[...]], axis=0)

    def score(b):
        keys = window(b, k_ref, upk, dnk, onk, twok, nextk)
        scores = lax.dot_general(
            q_ref[128 * b : 128 * (b + 1)], keys, NT, preferred_element_type=F32
        )
        (sa, sb)[b % 2][...] = scores

    def bias_of(b):
        g = b // 4
        fine = None
        if b == 0:
            fine = jnp.where(lane384 < 128, g_up, 0.0)
        if b == 7:
            fine = jnp.where(lane384 >= 256, g_dn, 0.0)
        if g == 0:
            edge1 = jnp.where(lane384 < 128, g_up, 0.0)
        else:
            edge1 = jnp.where(lane384 >= 256, g_dn, 0.0)
        start = 32 * (b % 4) + 96
        hidden = (lane384 >= start) & (lane384 < start + 96)
        inside = (token2 >= (g - 1) * HALF) & (token2 < (g + 2) * HALF)
        first = jnp.where(hidden, GONE, edge1) + 2.0 / c
        second = jnp.where(inside, GONE, edge2) + 4.0 / c
        return fine, first, second

    score(0)
    for b in range(8):
        if b < 7:
            score(b + 1)
        s_ref, p_ref = (sa, sb)[b % 2], (pa, pb)[b % 2]
        fine, first, second = bias_of(b)
        for r in range(8):
            rows = slice(16 * r, 16 * (r + 1))
            parts = []
            for j in range(9):
                t = s_ref[rows, 128 * j : 128 * (j + 1)]
                bias = (fine, first, second)[j // 3]
                if bias is not None:
                    t = t + bias[:, 128 * (j % 3) : 128 * (j % 3 + 1)]
                parts.append(t)
            top = jnp.max(functools.reduce(jnp.maximum, parts), axis=1, keepdims=True)
            for j, t in enumerate(parts):
                p_ref[rows, 128 * j : 128 * (j + 1)] = jnp.exp2((t - top) * c).astype(BF)
            ml_ref[128 * b + 16 * r : 128 * b + 16 * (r + 1)] = jnp.broadcast_to(
                top * c, (16, 128)
            )
        vals = window(b, v_ref, upv, dnv, onv, twov, nextv)
        both = jnp.dot(
            p_ref[...], jnp.concatenate([vals, ones], axis=1), preferred_element_type=F32
        )
        rows = slice(128 * b, 128 * (b + 1))
        acc_ref[rows] = both[:, :128]
        ml_ref[rows] = jnp.where(lane128 < 64, ml_ref[rows], both[:, 128:])


def near(pair, seq_size, dev, temp, queries, keys, values, up, down, one, two, beyond):
    smem = pl.BlockSpec(memory_space=pltpu.SMEM)

    def own(rows):
        return pl.BlockSpec((rows, HEAD_DIM), lambda i: (0, 2 * pair + i))

    def packed(rows):
        return [
            pl.BlockSpec((rows, HEAD_DIM), lambda i: (0, 4 * pair + i)),
            pl.BlockSpec((rows, HEAD_DIM), lambda i: (0, 4 * pair + 2 + i)),
        ]

    out = pl.BlockSpec((ROWS, HEAD_DIM), lambda i: (0, i))
    return pl.pallas_call(
        functools.partial(near_kernel, pair, seq_size),
        grid=(2,),
        in_specs=[smem, smem, own(ROWS), own(ROWS), own(ROWS)]
        + packed(256) + packed(256) + packed(256) + packed(256) + packed(128),
        out_specs=(out, out),
        out_shape=(sds((ROWS, PAIR), F32), sds((ROWS, PAIR), F32)),
        scratch_shapes=[pltpu.VMEM((128, 1152), F32)] * 2 + [pltpu.VMEM((128, 1152), BF)] * 2,
        compiler_params=params(),
        cost_estimate=cost(2_000_000_000, 6_000_000, 2_500_000),
    )(dev, temp, queries, keys, values, up, up, down, down, one, one, two, two, beyond, beyond)


CHUNK = 256


def far_kernel(
    pair, has_sum, dev_ref, temp_ref, q_ref, acc_ref, ml_ref, gain_ref, f0, f1, f2, f3, *rest
):
    if has_sum:
        before_ref, att_ref, sum_ref, sa, sb, pa, pb, a_ref = rest
    else:
        att_ref, sum_ref, sa, sb, pa, pb, a_ref = rest
    dev = dev_ref[0]
    y, own_pair = dev % Y, dev // 2
    lane = lax.broadcasted_iota(jnp.int32, (1, 256), 1)
    src_z = lane // 16
    biases = []
    for k in range(4):
        src_pair = (src_z * Y + (y + k) % Y) // 2
        seen = (src_pair < own_pair - 1) | (src_pair > own_pair + 1)
        biases.append(jnp.where(seen, 0.0, GONE).astype(F32))
    bias = jnp.concatenate(biases, axis=1)
    ones = jnp.ones((1024, 128), BF)
    starts = [0 if f.shape[1] == 512 else 512 * pair for f in (f0, f1, f2, f3)]
    blocks = list(zip((f0, f1, f2, f3), starts))

    def column(which, i):
        return jnp.concatenate(
            [
                f[:, at + PAIR * which + HEAD_DIM * i : at + PAIR * which + HEAD_DIM * (i + 1)]
                for f, at in blocks
            ],
            axis=0,
        )

    def part(step, carry):
        first = step * HALF

        def place(unit):
            return pl.ds(pl.multiple_of(first + CHUNK * (unit // 2), CHUNK), CHUNK)

        def score(unit):
            i = unit % 2
            q = q_ref[place(unit), PAIR * pair + HEAD_DIM * i : PAIR * pair + HEAD_DIM * (i + 1)]
            (sa, sb)[i][...] = lax.dot_general(
                q, column(0, i), NT, preferred_element_type=F32
            )

        squares = None
        score(0)
        for unit in range(4):
            if unit < 3:
                score(unit + 1)
            i = unit % 2
            c = temp_ref[2 * pair + i]
            cols = slice(HEAD_DIM * i, HEAD_DIM * (i + 1))
            s_ref, p_ref = (sa, sb)[i], (pa, pb)[i]
            shifted = bias + 6.0 / c
            start = first + CHUNK * (unit // 2)
            for r in range(CHUNK // 16):
                rows = slice(16 * r, 16 * (r + 1))
                parts = [
                    s_ref[rows, 128 * j : 128 * (j + 1)] + shifted[:, 128 * j : 128 * (j + 1)]
                    for j in range(8)
                ]
                best = jnp.max(functools.reduce(jnp.maximum, parts), axis=1, keepdims=True)
                there = pl.ds(pl.multiple_of(start + 16 * r, 16), 16)
                top_near = ml_ref[there, HEAD_DIM * i : HEAD_DIM * i + 1]
                top = jnp.maximum(top_near, c * best)
                for j, t in enumerate(parts):
                    p_ref[rows, 128 * j : 128 * (j + 1)] = jnp.exp2(c * t - top).astype(BF)
                a_ref[rows] = jnp.broadcast_to(jnp.exp2(top_near - top), (16, 128))
            both = jnp.dot(
                p_ref[...],
                jnp.concatenate([column(1, i), ones], axis=1),
                preferred_element_type=F32,
            )
            alpha = a_ref[...]
            here = place(unit)
            total = alpha * ml_ref[here, HEAD_DIM * i + 64 : HEAD_DIM * i + 65] + both[:, 128:]
            att = (acc_ref[here, cols] * alpha + both[:, :128]) / total
            att_ref[here, cols] = att * gain_ref[:, PAIR * pair + HEAD_DIM * i : PAIR * pair + HEAD_DIM * (i + 1)]
            if i == 0:
                squares = att * att
                continue
            squares = squares + att * att
            for j in range(CHUNK // 128):
                line = jnp.sum(
                    jnp.transpose(squares[128 * j : 128 * (j + 1)]), axis=0, keepdims=True
                )
                lanes = pl.ds(pl.multiple_of(start + 128 * j, 128), 128)
                if has_sum:
                    line = line + before_ref[:, lanes]
                sum_ref[:, lanes] = line
        return carry

    lax.fori_loop(0, 2, part, 0)


def far(pair, dev, temp, queries, acc, ml, gain, columns, before):
    smem = pl.BlockSpec(memory_space=pltpu.SMEM)
    whole = pl.BlockSpec(memory_space=pltpu.VMEM)
    extra = [] if before is None else [before]
    return pl.pallas_call(
        functools.partial(far_kernel, pair, before is not None),
        in_specs=[smem, smem] + [whole] * (8 + len(extra)),
        out_specs=(whole, whole),
        out_shape=(sds((ROWS, PAIR), F32), sds((1, ROWS), F32)),
        scratch_shapes=[pltpu.VMEM((CHUNK, 1024), F32)] * 2
        + [pltpu.VMEM((CHUNK, 1024), BF)] * 2
        + [pltpu.VMEM((CHUNK, 128), F32)],
        compiler_params=params(),
        cost_estimate=cost(1_200_000_000, 5_000_000, 2_100_000),
    )(dev, temp, queries, acc, ml, gain, *columns, *extra)


def norm_kernel(a_ref, b_ref, sum_ref, out_ref):
    start = pl.program_id(0) * CHUNK
    for j in range(CHUNK // 128):
        rows = slice(128 * j, 128 * (j + 1))
        there = pl.ds(pl.multiple_of(start + 128 * j, 128), 128)
        mean = jnp.sum(sum_ref[:, there], axis=0, keepdims=True) / (HEADS * HEAD_DIM)
        inverse = lax.rsqrt(mean + EPS)
        tall = jnp.transpose(jnp.broadcast_to(inverse, (128, 128)))
        for h in range(4):
            ref = a_ref if h < 2 else b_ref
            cols = slice(HEAD_DIM * (h % 2), HEAD_DIM * (h % 2 + 1))
            to = slice(HEAD_DIM * h, HEAD_DIM * (h + 1))
            out_ref[rows, to] = (ref[there, cols] * tall).astype(BF)


def norm(att_a, att_b, sums):
    whole = pl.BlockSpec(memory_space=pltpu.VMEM)
    return pl.pallas_call(
        norm_kernel,
        grid=(ROWS // CHUNK,),
        in_specs=[whole, whole, whole],
        out_specs=pl.BlockSpec((CHUNK, 512), lambda i: (i, 0)),
        out_shape=sds((ROWS, 512), BF),
        compiler_params=params(),
        cost_estimate=cost(2_000_000, 3_000_000),
    )(att_a, att_b, sums)


def fetch(value, axis, source):
    count = lax.axis_size(axis)
    return lax.ppermute(value, axis, [(source(i) % count, i) for i in range(count)])


def fetch_y(value, step):
    return fetch(value, "seq", lambda i: i // Y * Y + (i + step) % Y)


def gathered(value, axis):
    size = lax.axis_size(axis)
    many = jnp.broadcast_to(value[None], (size,) + value.shape)
    return lax.all_to_all(many, axis, 0, 0, tiled=True)


Y_RING = [[z * Y + y for y in range(Y)] for z in range(Z)]
Z_RING = [[z * Y + y for z in range(Z)] for y in range(Y)]


def joined(value, groups):
    return lax.all_gather(value, "seq", axis_index_groups=groups, axis=0, tiled=True)


def local(queries, keys, values, head_temp, norm_gain):
    seq_size = lax.axis_size("seq")
    dev = lax.axis_index("seq").astype(jnp.int32).reshape(1)
    temp = head_temp * F32(math.log2(math.e) / math.sqrt(HEAD_DIM))
    up, down, one, two, three = prep(keys, values)

    group_two = joined(two, Y_RING)
    up, down, three, group_two = lax.optimization_barrier((up, down, three, group_two))
    from_up = fetch(up, "seq", lambda i: i - 1)
    from_down = fetch(down, "seq", lambda i: i + 1)
    low_side = dev[0] % Y < 2
    other_half = jnp.where(low_side, group_two[128:], group_two[:128])
    beyond = fetch(other_half, "seq", lambda i: i - Y if i % Y < 2 else i + Y)

    column = joined(three, Z_RING)
    near_args = (queries, keys, values, from_up, from_down, one, group_two, beyond)
    acc_a, ml_a = near(0, seq_size, dev, temp, *near_args)
    acc_b, ml_b = near(1, seq_size, dev, temp, *near_args)
    column, acc_a, ml_a = lax.optimization_barrier((column, acc_a, ml_a))
    after = fetch_y(column, 1)
    before = fetch_y(column, -1)
    half_a, half_b, acc_b, ml_b = lax.optimization_barrier(
        (after[:, :512], before[:, 512:], acc_b, ml_b)
    )
    opposite_a = fetch_y(half_a, 1)
    opposite_b = fetch_y(half_b, -1)

    gain = norm_gain.reshape(1, 512)
    att_a, sum_a = far(0, dev, temp, queries, acc_a, ml_a, gain, (column, after, opposite_a, before), None)
    att_b, sums = far(1, dev, temp, queries, acc_b, ml_b, gain, (column, after, opposite_b, before), sum_a)
    sums = gathered(sums, "head").reshape(8, ROWS)
    return norm(att_a, att_b, sums)


def solution(mesh):
    return jax.shard_map(
        local,
        mesh=mesh,
        in_specs=(P("seq", "head"), P("seq", "head"), P("seq", "head"), P("head"), P("head")),
        out_specs=P("seq", "head"),
        check_vma=False,
    )
```

```python
import functools
import math

import jax
import jax.numpy as jnp
from jax import lax
from jax.experimental import pallas as pl
from jax.experimental.pallas import tpu as pltpu
from jax.sharding import PartitionSpec as P

HEADS = 32
HEAD_DIM = 128
BLK = 128
ROWS = 1024
HALF = 512
PAIR = 2 * HEAD_DIM
Y = 4
Z = 16

EPS = 1e-06
GONE = -1e30
NT = (((1,), (1,)), ((), ()))
BF = jnp.bfloat16
F32 = jnp.float32
VMEM_LIMIT = 48 * 1024 * 1024


def params():
    return pltpu.CompilerParams(vmem_limit_bytes=VMEM_LIMIT)


def cost(flops, moved, exps=0):
    return pl.CostEstimate(flops=flops, bytes_accessed=moved, transcendentals=exps)


def sds(shape, dtype):
    return jax.ShapeDtypeStruct(shape, dtype)


def prep_kernel(k_ref, v_ref, up_ref, down_ref, one_ref, two_ref, three_ref):
    rows = lax.broadcasted_iota(jnp.int32, (64, 256), 0)
    cols = lax.broadcasted_iota(jnp.int32, (64, 256), 1)
    pool = jnp.where(cols // 4 == rows, 0.25, 0.0).astype(BF)
    for which, ref in ((0, k_ref), (1, v_ref)):
        for pair in range(2):
            src = slice(pair * PAIR, (pair + 1) * PAIR)
            to = slice((2 * pair + which) * PAIR, (2 * pair + which + 1) * PAIR)
            for j in range(4):
                part = jnp.dot(pool, ref[256 * j : 256 * (j + 1), src], preferred_element_type=F32)
                one_ref[64 * j : 64 * (j + 1), to] = part.astype(BF)
            two = jnp.dot(pool, one_ref[:, to], preferred_element_type=F32).astype(BF)
            three = jnp.dot(pool[:16, :64], two, preferred_element_type=F32).astype(BF)
            two_ref[:, to] = two
            three_ref[:, to] = three
            up_ref[0:128, to] = ref[ROWS - 128 : ROWS, src]
            up_ref[128:256, to] = one_ref[128:256, to]
            down_ref[0:128, to] = ref[0:128, src]
            down_ref[128:256, to] = one_ref[0:128, to]


def prep(keys, values):
    return pl.pallas_call(
        prep_kernel,
        out_shape=(
            sds((256, 1024), BF),
            sds((256, 1024), BF),
            sds((256, 1024), BF),
            sds((64, 1024), BF),
            sds((16, 1024), BF),
        ),
        compiler_params=params(),
        cost_estimate=cost(700_000_000, 5_000_000),
    )(keys, values)


def near_kernel(pair, seq_size, *refs):
    for i in range(2):
        near_head(pair, seq_size, i, *refs)


def near_head(
    pair, seq_size, i, dev_ref, temp_ref, q_all, k_all, v_all, up_all, down_all, one_all, two_all,
    next_all, acc_all, ml_all, sa, sb, pa, pb,
):
    def head_cols(ref, first):
        return ref.at[:, HEAD_DIM * (first + i) : HEAD_DIM * (first + i + 1)]

    q_ref, k_ref, v_ref = [head_cols(ref, 2 * pair) for ref in (q_all, k_all, v_all)]
    acc_ref, ml_ref = head_cols(acc_all, 0), head_cols(ml_all, 0)
    edges = (up_all, down_all, one_all, two_all, next_all)
    upk, dnk, onk, twok, nextk = [head_cols(ref, 4 * pair) for ref in edges]
    upv, dnv, onv, twov, nextv = [head_cols(ref, 4 * pair + 2) for ref in edges]
    dev = dev_ref[0]
    c = temp_ref[2 * pair + i]
    z, y = dev // Y, dev % Y

    def gate(ok):
        return jnp.where(ok, 0.0, GONE).astype(F32)

    g_up = gate(dev >= 1)
    g_dn = gate(dev <= seq_size - 2)
    g_next = jnp.where(y < 2, gate(z >= 1), gate(z <= seq_size // Y - 2))

    lane384 = lax.broadcasted_iota(jnp.int32, (1, 384), 1)
    lane128 = lax.broadcasted_iota(jnp.int32, (128, 128), 1)
    ones = jnp.ones((1152, 128), BF)
    next_first = jnp.where(y < 2, -2 * ROWS, 4 * ROWS) - 256 * 16
    token2 = lane384 * 16 - y * ROWS + jnp.where(lane384 < 256, 0, next_first)
    edge2 = jnp.where(lane384 < 256, 0.0, g_next)

    def window(b, own_ref, up_ref, dn_ref, one_ref, two_ref, next_ref):
        if b == 0:
            fine = [up_ref[0:128], own_ref[0:256]]
        elif b == 7:
            fine = [own_ref[768:1024], dn_ref[0:128]]
        else:
            fine = [own_ref[128 * (b - 1) : 128 * (b + 2)]]
        if b < 4:
            first = [up_ref[128:256], one_ref[...]]
        else:
            first = [one_ref[...], dn_ref[128:256]]
        return jnp.concatenate(fine + first + [two_ref[...], next_ref[...]], axis=0)

    def score(b):
        keys = window(b, k_ref, upk, dnk, onk, twok, nextk)
        scores = lax.dot_general(
            q_ref[128 * b : 128 * (b + 1)], keys, NT, preferred_element_type=F32
        )
        (sa, sb)[b % 2][...] = scores

    def bias_of(b):
        g = b // 4
        fine = None
        if b == 0:
            fine = jnp.where(lane384 < 128, g_up, 0.0)
        if b == 7:
            fine = jnp.where(lane384 >= 256, g_dn, 0.0)
        if g == 0:
            edge1 = jnp.where(lane384 < 128, g_up, 0.0)
        else:
            edge1 = jnp.where(lane384 >= 256, g_dn, 0.0)
        start = 32 * (b % 4) + 96
        hidden = (lane384 >= start) & (lane384 < start + 96)
        inside = (token2 >= (g - 1) * HALF) & (token2 < (g + 2) * HALF)
        first = jnp.where(hidden, GONE, edge1) + 2.0 / c
        second = jnp.where(inside, GONE, edge2) + 4.0 / c
        return fine, first, second

    score(0)
    for b in range(8):
        if b < 7:
            score(b + 1)
        s_ref, p_ref = (sa, sb)[b % 2], (pa, pb)[b % 2]
        fine, first, second = bias_of(b)
        for r in range(8):
            rows = slice(16 * r, 16 * (r + 1))
            parts = []
            for j in range(9):
                t = s_ref[rows, 128 * j : 128 * (j + 1)]
                bias = (fine, first, second)[j // 3]
                if bias is not None:
                    t = t + bias[:, 128 * (j % 3) : 128 * (j % 3 + 1)]
                parts.append(t)
            top = jnp.max(functools.reduce(jnp.maximum, parts), axis=1, keepdims=True)
            for j, t in enumerate(parts):
                p_ref[rows, 128 * j : 128 * (j + 1)] = jnp.exp2((t - top) * c).astype(BF)
            ml_ref[128 * b + 16 * r : 128 * b + 16 * (r + 1)] = jnp.broadcast_to(
                top * c, (16, 128)
            )
        vals = window(b, v_ref, upv, dnv, onv, twov, nextv)
        both = jnp.dot(
            p_ref[...], jnp.concatenate([vals, ones], axis=1), preferred_element_type=F32
        )
        rows = slice(128 * b, 128 * (b + 1))
        acc_ref[rows] = both[:, :128]
        ml_ref[rows] = jnp.where(lane128 < 64, ml_ref[rows], both[:, 128:])


def near(pair, seq_size, dev, temp, queries, keys, values, up, down, one, two, beyond):
    smem = pl.BlockSpec(memory_space=pltpu.SMEM)

    whole = pl.BlockSpec(memory_space=pltpu.VMEM)
    return pl.pallas_call(
        functools.partial(near_kernel, pair, seq_size),
        in_specs=[smem, smem] + [whole] * 8,
        out_specs=(whole, whole),
        out_shape=(sds((ROWS, PAIR), F32), sds((ROWS, PAIR), F32)),
        scratch_shapes=[pltpu.VMEM((128, 1152), F32)] * 2 + [pltpu.VMEM((128, 1152), BF)] * 2,
        compiler_params=params(),
        cost_estimate=cost(2_000_000_000, 6_000_000, 2_500_000),
    )(dev, temp, queries, keys, values, up, down, one, two, beyond)


CHUNK = 256


def far_kernel(
    pair, has_sum, dev_ref, temp_ref, q_ref, acc_ref, ml_ref, gain_ref, f0, f1, f2, f3, *rest
):
    if has_sum:
        before_ref, att_ref, sum_ref, sa, sb, pa, pb, a_ref = rest
    else:
        att_ref, sum_ref, sa, sb, pa, pb, a_ref = rest
    dev = dev_ref[0]
    y, own_pair = dev % Y, dev // 2
    lane = lax.broadcasted_iota(jnp.int32, (1, 256), 1)
    src_z = lane // 16
    biases = []
    for k in range(4):
        src_pair = (src_z * Y + (y + k) % Y) // 2
        seen = (src_pair < own_pair - 1) | (src_pair > own_pair + 1)
        biases.append(jnp.where(seen, 0.0, GONE).astype(F32))
    bias = jnp.concatenate(biases, axis=1)
    ones = jnp.ones((1024, 128), BF)
    starts = [0 if f.shape[1] == 512 else 512 * pair for f in (f0, f1, f2, f3)]
    blocks = list(zip((f0, f1, f2, f3), starts))

    def column(which, i):
        return jnp.concatenate(
            [
                f[:, at + PAIR * which + HEAD_DIM * i : at + PAIR * which + HEAD_DIM * (i + 1)]
                for f, at in blocks
            ],
            axis=0,
        )

    def part(step, carry):
        first = step * HALF

        def place(unit):
            return pl.ds(pl.multiple_of(first + CHUNK * (unit // 2), CHUNK), CHUNK)

        def score(unit):
            i = unit % 2
            q = q_ref[place(unit), PAIR * pair + HEAD_DIM * i : PAIR * pair + HEAD_DIM * (i + 1)]
            (sa, sb)[i][...] = lax.dot_general(
                q, column(0, i), NT, preferred_element_type=F32
            )

        squares = None
        score(0)
        for unit in range(4):
            if unit < 3:
                score(unit + 1)
            i = unit % 2
            c = temp_ref[2 * pair + i]
            cols = slice(HEAD_DIM * i, HEAD_DIM * (i + 1))
            s_ref, p_ref = (sa, sb)[i], (pa, pb)[i]
            shifted = bias + 6.0 / c
            start = first + CHUNK * (unit // 2)
            for r in range(CHUNK // 16):
                rows = slice(16 * r, 16 * (r + 1))
                parts = [
                    s_ref[rows, 128 * j : 128 * (j + 1)] + shifted[:, 128 * j : 128 * (j + 1)]
                    for j in range(8)
                ]
                best = jnp.max(functools.reduce(jnp.maximum, parts), axis=1, keepdims=True)
                there = pl.ds(pl.multiple_of(start + 16 * r, 16), 16)
                top_near = ml_ref[there, HEAD_DIM * i : HEAD_DIM * i + 1]
                top = jnp.maximum(top_near, c * best)
                for j, t in enumerate(parts):
                    p_ref[rows, 128 * j : 128 * (j + 1)] = jnp.exp2(c * t - top).astype(BF)
                a_ref[rows] = jnp.broadcast_to(jnp.exp2(top_near - top), (16, 128))
            both = jnp.dot(
                p_ref[...],
                jnp.concatenate([column(1, i), ones], axis=1),
                preferred_element_type=F32,
            )
            alpha = a_ref[...]
            here = place(unit)
            total = alpha * ml_ref[here, HEAD_DIM * i + 64 : HEAD_DIM * i + 65] + both[:, 128:]
            att = (acc_ref[here, cols] * alpha + both[:, :128]) / total
            att_ref[here, cols] = att * gain_ref[:, PAIR * pair + HEAD_DIM * i : PAIR * pair + HEAD_DIM * (i + 1)]
            if i == 0:
                squares = att * att
                continue
            squares = squares + att * att
            for j in range(CHUNK // 128):
                line = jnp.sum(
                    jnp.transpose(squares[128 * j : 128 * (j + 1)]), axis=0, keepdims=True
                )
                lanes = pl.ds(pl.multiple_of(start + 128 * j, 128), 128)
                if has_sum:
                    line = line + before_ref[:, lanes]
                sum_ref[:, lanes] = line
        return carry

    lax.fori_loop(0, 2, part, 0)


def far(pair, dev, temp, queries, acc, ml, gain, columns, before):
    smem = pl.BlockSpec(memory_space=pltpu.SMEM)
    whole = pl.BlockSpec(memory_space=pltpu.VMEM)
    extra = [] if before is None else [before]
    return pl.pallas_call(
        functools.partial(far_kernel, pair, before is not None),
        in_specs=[smem, smem] + [whole] * (8 + len(extra)),
        out_specs=(whole, whole),
        out_shape=(sds((ROWS, PAIR), F32), sds((1, ROWS), F32)),
        scratch_shapes=[pltpu.VMEM((CHUNK, 1024), F32)] * 2
        + [pltpu.VMEM((CHUNK, 1024), BF)] * 2
        + [pltpu.VMEM((CHUNK, 128), F32)],
        compiler_params=params(),
        cost_estimate=cost(1_200_000_000, 5_000_000, 2_100_000),
    )(dev, temp, queries, acc, ml, gain, *columns, *extra)


def norm_kernel(a_ref, b_ref, sum_ref, out_ref):
    start = pl.program_id(0) * CHUNK
    for j in range(CHUNK // 128):
        rows = slice(128 * j, 128 * (j + 1))
        there = pl.ds(pl.multiple_of(start + 128 * j, 128), 128)
        mean = jnp.sum(sum_ref[:, there], axis=0, keepdims=True) / (HEADS * HEAD_DIM)
        inverse = lax.rsqrt(mean + EPS)
        tall = jnp.transpose(jnp.broadcast_to(inverse, (128, 128)))
        for h in range(4):
            ref = a_ref if h < 2 else b_ref
            cols = slice(HEAD_DIM * (h % 2), HEAD_DIM * (h % 2 + 1))
            to = slice(HEAD_DIM * h, HEAD_DIM * (h + 1))
            out_ref[rows, to] = (ref[there, cols] * tall).astype(BF)


def norm(att_a, att_b, sums):
    whole = pl.BlockSpec(memory_space=pltpu.VMEM)
    return pl.pallas_call(
        norm_kernel,
        grid=(ROWS // CHUNK,),
        in_specs=[whole, whole, whole],
        out_specs=pl.BlockSpec((CHUNK, 512), lambda i: (i, 0)),
        out_shape=sds((ROWS, 512), BF),
        compiler_params=params(),
        cost_estimate=cost(2_000_000, 3_000_000),
    )(att_a, att_b, sums)


def fetch(value, axis, source):
    count = lax.axis_size(axis)
    return lax.ppermute(value, axis, [(source(i) % count, i) for i in range(count)])


def fetch_y(value, step):
    return fetch(value, "seq", lambda i: i // Y * Y + (i + step) % Y)


def gathered(value, axis):
    size = lax.axis_size(axis)
    many = jnp.broadcast_to(value[None], (size,) + value.shape)
    return lax.all_to_all(many, axis, 0, 0, tiled=True)


Y_RING = [[z * Y + y for y in range(Y)] for z in range(Z)]
Z_RING = [[z * Y + y for z in range(Z)] for y in range(Y)]


def joined(value, groups):
    rows, columns = value.shape
    tiles = value.reshape(rows // 8, 8, columns)
    blocks = lax.all_gather(tiles, "seq", axis_index_groups=groups, axis=0, tiled=True)
    return blocks.reshape(len(groups[0]) * rows, columns)


def local(queries, keys, values, head_temp, norm_gain):
    seq_size = lax.axis_size("seq")
    dev = lax.axis_index("seq").astype(jnp.int32).reshape(1)
    temp = head_temp * F32(math.log2(math.e) / math.sqrt(HEAD_DIM))
    up, down, one, two, three = prep(keys, values)

    group_two = joined(two, Y_RING)
    up, down, three, group_two = lax.optimization_barrier((up, down, three, group_two))
    from_up = fetch(up, "seq", lambda i: i - 1)
    from_down = fetch(down, "seq", lambda i: i + 1)
    low_side = dev[0] % Y < 2
    other_half = jnp.where(low_side, group_two[128:], group_two[:128])
    beyond = fetch(other_half, "seq", lambda i: i - Y if i % Y < 2 else i + Y)

    column = joined(three, Z_RING)
    near_args = (queries, keys, values, from_up, from_down, one, group_two, beyond)
    acc_a, ml_a = near(0, seq_size, dev, temp, *near_args)
    acc_b, ml_b = near(1, seq_size, dev, temp, *near_args)
    column, acc_a, ml_a = lax.optimization_barrier((column, acc_a, ml_a))
    after = fetch_y(column, 1)
    before = fetch_y(column, -1)
    half_a, half_b, acc_b, ml_b = lax.optimization_barrier(
        (after[:, :512], before[:, 512:], acc_b, ml_b)
    )
    opposite_a = fetch_y(half_a, 1)
    opposite_b = fetch_y(half_b, -1)

    gain = norm_gain.reshape(1, 512)
    att_a, sum_a = far(0, dev, temp, queries, acc_a, ml_a, gain, (column, after, opposite_a, before), None)
    att_b, sums = far(1, dev, temp, queries, acc_b, ml_b, gain, (column, after, opposite_b, before), sum_a)
    sums = gathered(sums, "head").reshape(8, ROWS)
    return norm(att_a, att_b, sums)


def solution(mesh):
    return jax.shard_map(
        local,
        mesh=mesh,
        in_specs=(P("seq", "head"), P("seq", "head"), P("seq", "head"), P("head"), P("head")),
        out_specs=P("seq", "head"),
        check_vma=False,
    )
```

```python
import functools
import math

import jax
import jax.numpy as jnp
from jax import lax
from jax.experimental import pallas as pl
from jax.experimental.pallas import tpu as pltpu
from jax.sharding import PartitionSpec as P

HEADS = 32
HEAD_DIM = 128
BLK = 128
ROWS = 1024
HALF = 512
PAIR = 2 * HEAD_DIM
Y = 4
Z = 16

EPS = 1e-06
GONE = -1e30
NT = (((1,), (1,)), ((), ()))
BF = jnp.bfloat16
F32 = jnp.float32
VMEM_LIMIT = 48 * 1024 * 1024


def params():
    return pltpu.CompilerParams(vmem_limit_bytes=VMEM_LIMIT)


def cost(flops, moved, exps=0):
    return pl.CostEstimate(flops=flops, bytes_accessed=moved, transcendentals=exps)


def sds(shape, dtype):
    return jax.ShapeDtypeStruct(shape, dtype)


def prep_kernel(k_ref, v_ref, up_ref, down_ref, one_ref, two_ref, three_ref):
    rows = lax.broadcasted_iota(jnp.int32, (64, 256), 0)
    cols = lax.broadcasted_iota(jnp.int32, (64, 256), 1)
    pool = jnp.where(cols // 4 == rows, 0.25, 0.0).astype(BF)
    for which, ref in ((0, k_ref), (1, v_ref)):
        for pair in range(2):
            src = slice(pair * PAIR, (pair + 1) * PAIR)
            to = slice((2 * pair + which) * PAIR, (2 * pair + which + 1) * PAIR)
            for j in range(4):
                part = jnp.dot(pool, ref[256 * j : 256 * (j + 1), src], preferred_element_type=F32)
                one_ref[64 * j : 64 * (j + 1), to] = part.astype(BF)
            two = jnp.dot(pool, one_ref[:, to], preferred_element_type=F32).astype(BF)
            three = jnp.dot(pool[:16, :64], two, preferred_element_type=F32).astype(BF)
            two_ref[:, to] = two
            three_ref[:, to] = three
            up_ref[0:128, to] = ref[ROWS - 128 : ROWS, src]
            up_ref[128:256, to] = one_ref[128:256, to]
            down_ref[0:128, to] = ref[0:128, src]
            down_ref[128:256, to] = one_ref[0:128, to]


def prep(keys, values):
    return pl.pallas_call(
        prep_kernel,
        out_shape=(
            sds((256, 1024), BF),
            sds((256, 1024), BF),
            sds((256, 1024), BF),
            sds((64, 1024), BF),
            sds((16, 1024), BF),
        ),
        compiler_params=params(),
        cost_estimate=cost(700_000_000, 5_000_000),
    )(keys, values)


def near_kernel(
    pair, seq_size, dev_ref, temp_ref, q_ref, k_ref, v_ref,
    upk, upv, dnk, dnv, onk, onv, twok, twov, nextk, nextv,
    acc_ref, ml_ref, sa, sb, pa, pb,
):
    dev = dev_ref[0]
    c = temp_ref[2 * pair + pl.program_id(0)]
    z, y = dev // Y, dev % Y

    def gate(ok):
        return jnp.where(ok, 0.0, GONE).astype(F32)

    g_up = gate(dev >= 1)
    g_dn = gate(dev <= seq_size - 2)
    g_next = jnp.where(y < 2, gate(z >= 1), gate(z <= seq_size // Y - 2))

    lane384 = lax.broadcasted_iota(jnp.int32, (1, 384), 1)
    lane128 = lax.broadcasted_iota(jnp.int32, (128, 128), 1)
    ones = jnp.ones((1152, 128), BF)
    next_first = jnp.where(y < 2, -2 * ROWS, 4 * ROWS) - 256 * 16
    token2 = lane384 * 16 - y * ROWS + jnp.where(lane384 < 256, 0, next_first)
    edge2 = jnp.where(lane384 < 256, 0.0, g_next)

    def window(b, own_ref, up_ref, dn_ref, one_ref, two_ref, next_ref):
        if b == 0:
            fine = [up_ref[0:128], own_ref[0:256]]
        elif b == 7:
            fine = [own_ref[768:1024], dn_ref[0:128]]
        else:
            fine = [own_ref[128 * (b - 1) : 128 * (b + 2)]]
        if b < 4:
            first = [up_ref[128:256], one_ref[...]]
        else:
            first = [one_ref[...], dn_ref[128:256]]
        return jnp.concatenate(fine + first + [two_ref[...], next_ref[...]], axis=0)

    def score(b):
        keys = window(b, k_ref, upk, dnk, onk, twok, nextk)
        scores = lax.dot_general(
            q_ref[128 * b : 128 * (b + 1)], keys, NT, preferred_element_type=F32
        )
        (sa, sb)[b % 2][...] = scores

    def bias_of(b):
        g = b // 4
        fine = None
        if b == 0:
            fine = jnp.where(lane384 < 128, g_up, 0.0)
        if b == 7:
            fine = jnp.where(lane384 >= 256, g_dn, 0.0)
        if g == 0:
            edge1 = jnp.where(lane384 < 128, g_up, 0.0)
        else:
            edge1 = jnp.where(lane384 >= 256, g_dn, 0.0)
        start = 32 * (b % 4) + 96
        hidden = (lane384 >= start) & (lane384 < start + 96)
        inside = (token2 >= (g - 1) * HALF) & (token2 < (g + 2) * HALF)
        first = jnp.where(hidden, GONE, edge1) + 2.0 / c
        second = jnp.where(inside, GONE, edge2) + 4.0 / c
        return fine, first, second

    score(0)
    for b in range(8):
        if b < 7:
            score(b + 1)
        s_ref, p_ref = (sa, sb)[b % 2], (pa, pb)[b % 2]
        fine, first, second = bias_of(b)
        for r in range(8):
            rows = slice(16 * r, 16 * (r + 1))
            parts = []
            for j in range(9):
                t = s_ref[rows, 128 * j : 128 * (j + 1)]
                bias = (fine, first, second)[j // 3]
                if bias is not None:
                    t = t + bias[:, 128 * (j % 3) : 128 * (j % 3 + 1)]
                parts.append(t)
            top = jnp.max(functools.reduce(jnp.maximum, parts), axis=1, keepdims=True)
            for j, t in enumerate(parts):
                p_ref[rows, 128 * j : 128 * (j + 1)] = jnp.exp2((t - top) * c).astype(BF)
            ml_ref[128 * b + 16 * r : 128 * b + 16 * (r + 1)] = jnp.broadcast_to(
                top * c, (16, 128)
            )
        vals = window(b, v_ref, upv, dnv, onv, twov, nextv)
        both = jnp.dot(
            p_ref[...], jnp.concatenate([vals, ones], axis=1), preferred_element_type=F32
        )
        rows = slice(128 * b, 128 * (b + 1))
        acc_ref[rows] = both[:, :128]
        ml_ref[rows] = jnp.where(lane128 < 64, ml_ref[rows], both[:, 128:])


def near(pair, seq_size, dev, temp, queries, keys, values, up, down, one, two, beyond):
    smem = pl.BlockSpec(memory_space=pltpu.SMEM)

    def own(rows):
        return pl.BlockSpec((rows, HEAD_DIM), lambda i: (0, 2 * pair + i))

    def packed(rows):
        return [
            pl.BlockSpec((rows, HEAD_DIM), lambda i: (0, 4 * pair + i)),
            pl.BlockSpec((rows, HEAD_DIM), lambda i: (0, 4 * pair + 2 + i)),
        ]

    out = pl.BlockSpec((ROWS, HEAD_DIM), lambda i: (0, i))
    return pl.pallas_call(
        functools.partial(near_kernel, pair, seq_size),
        grid=(2,),
        in_specs=[smem, smem, own(ROWS), own(ROWS), own(ROWS)]
        + packed(256) + packed(256) + packed(256) + packed(256) + packed(128),
        out_specs=(out, out),
        out_shape=(sds((ROWS, PAIR), F32), sds((ROWS, PAIR), F32)),
        scratch_shapes=[pltpu.VMEM((128, 1152), F32)] * 2 + [pltpu.VMEM((128, 1152), BF)] * 2,
        compiler_params=params(),
        cost_estimate=cost(2_000_000_000, 6_000_000, 2_500_000),
    )(dev, temp, queries, keys, values, up, up, down, down, one, one, two, two, beyond, beyond)


CHUNK = 256


def far_kernel(
    pair, has_sum, dev_ref, temp_ref, q_ref, acc_ref, ml_ref, gain_ref, f0, f1, f2, f3, *rest
):
    if has_sum:
        before_ref, att_ref, sum_ref, sa, sb, pa, pb, a_ref = rest
    else:
        att_ref, sum_ref, sa, sb, pa, pb, a_ref = rest
    dev = dev_ref[0]
    y, own_pair = dev % Y, dev // 2
    lane = lax.broadcasted_iota(jnp.int32, (1, 256), 1)
    src_z = lane // 16
    biases = []
    for k in range(4):
        src_pair = (src_z * Y + (y + k) % Y) // 2
        seen = (src_pair < own_pair - 1) | (src_pair > own_pair + 1)
        biases.append(jnp.where(seen, 0.0, GONE).astype(F32))
    bias = jnp.concatenate(biases, axis=1)
    ones = jnp.ones((1024, 128), BF)
    starts = [0 if f.shape[1] == 512 else 512 * pair for f in (f0, f1, f2, f3)]
    blocks = list(zip((f0, f1, f2, f3), starts))

    def column(which, i):
        return jnp.concatenate(
            [
                f[:, at + PAIR * which + HEAD_DIM * i : at + PAIR * which + HEAD_DIM * (i + 1)]
                for f, at in blocks
            ],
            axis=0,
        )

    def part(step, carry):
        first = step * HALF

        def place(unit):
            return pl.ds(pl.multiple_of(first + CHUNK * (unit // 2), CHUNK), CHUNK)

        def score(unit):
            i = unit % 2
            q = q_ref[place(unit), PAIR * pair + HEAD_DIM * i : PAIR * pair + HEAD_DIM * (i + 1)]
            (sa, sb)[i][...] = lax.dot_general(
                q, column(0, i), NT, preferred_element_type=F32
            )

        squares = None
        score(0)
        for unit in range(4):
            if unit < 3:
                score(unit + 1)
            i = unit % 2
            c = temp_ref[2 * pair + i]
            cols = slice(HEAD_DIM * i, HEAD_DIM * (i + 1))
            s_ref, p_ref = (sa, sb)[i], (pa, pb)[i]
            shifted = bias + 6.0 / c
            start = first + CHUNK * (unit // 2)
            for r in range(CHUNK // 16):
                rows = slice(16 * r, 16 * (r + 1))
                parts = [
                    s_ref[rows, 128 * j : 128 * (j + 1)] + shifted[:, 128 * j : 128 * (j + 1)]
                    for j in range(8)
                ]
                best = jnp.max(functools.reduce(jnp.maximum, parts), axis=1, keepdims=True)
                there = pl.ds(pl.multiple_of(start + 16 * r, 16), 16)
                top_near = ml_ref[there, HEAD_DIM * i : HEAD_DIM * i + 1]
                top = jnp.maximum(top_near, c * best)
                for j, t in enumerate(parts):
                    p_ref[rows, 128 * j : 128 * (j + 1)] = jnp.exp2(c * t - top).astype(BF)
                a_ref[rows] = jnp.broadcast_to(jnp.exp2(top_near - top), (16, 128))
            both = jnp.dot(
                p_ref[...],
                jnp.concatenate([column(1, i), ones], axis=1),
                preferred_element_type=F32,
            )
            alpha = a_ref[...]
            here = place(unit)
            total = alpha * ml_ref[here, HEAD_DIM * i + 64 : HEAD_DIM * i + 65] + both[:, 128:]
            att = (acc_ref[here, cols] * alpha + both[:, :128]) / total
            att_ref[here, cols] = att * gain_ref[:, PAIR * pair + HEAD_DIM * i : PAIR * pair + HEAD_DIM * (i + 1)]
            if i == 0:
                squares = att * att
                continue
            squares = squares + att * att
            for j in range(CHUNK // 128):
                line = jnp.sum(
                    jnp.transpose(squares[128 * j : 128 * (j + 1)]), axis=0, keepdims=True
                )
                lanes = pl.ds(pl.multiple_of(start + 128 * j, 128), 128)
                if has_sum:
                    line = line + before_ref[:, lanes]
                sum_ref[:, lanes] = line
        return carry

    lax.fori_loop(0, 2, part, 0)


def far(pair, dev, temp, queries, acc, ml, gain, columns, before):
    smem = pl.BlockSpec(memory_space=pltpu.SMEM)
    whole = pl.BlockSpec(memory_space=pltpu.VMEM)
    extra = [] if before is None else [before]
    return pl.pallas_call(
        functools.partial(far_kernel, pair, before is not None),
        in_specs=[smem, smem] + [whole] * (8 + len(extra)),
        out_specs=(whole, whole),
        out_shape=(sds((ROWS, PAIR), F32), sds((1, ROWS), F32)),
        scratch_shapes=[pltpu.VMEM((CHUNK, 1024), F32)] * 2
        + [pltpu.VMEM((CHUNK, 1024), BF)] * 2
        + [pltpu.VMEM((CHUNK, 128), F32)],
        compiler_params=params(),
        cost_estimate=cost(1_200_000_000, 5_000_000, 2_100_000),
    )(dev, temp, queries, acc, ml, gain, *columns, *extra)


def norm_kernel(a_ref, b_ref, sum_ref, out_ref):
    start = pl.program_id(0) * CHUNK
    for j in range(CHUNK // 128):
        rows = slice(128 * j, 128 * (j + 1))
        there = pl.ds(pl.multiple_of(start + 128 * j, 128), 128)
        mean = jnp.sum(sum_ref[:, there], axis=0, keepdims=True) / (HEADS * HEAD_DIM)
        inverse = lax.rsqrt(mean + EPS)
        tall = jnp.transpose(jnp.broadcast_to(inverse, (128, 128)))
        for h in range(4):
            ref = a_ref if h < 2 else b_ref
            cols = slice(HEAD_DIM * (h % 2), HEAD_DIM * (h % 2 + 1))
            to = slice(HEAD_DIM * h, HEAD_DIM * (h + 1))
            out_ref[rows, to] = (ref[there, cols] * tall).astype(BF)


def norm(att_a, att_b, sums):
    whole = pl.BlockSpec(memory_space=pltpu.VMEM)
    return pl.pallas_call(
        norm_kernel,
        grid=(ROWS // CHUNK,),
        in_specs=[whole, whole, whole],
        out_specs=pl.BlockSpec((CHUNK, 512), lambda i: (i, 0)),
        out_shape=sds((ROWS, 512), BF),
        compiler_params=params(),
        cost_estimate=cost(2_000_000, 3_000_000),
    )(att_a, att_b, sums)


def fetch(value, axis, source):
    count = lax.axis_size(axis)
    return lax.ppermute(value, axis, [(source(i) % count, i) for i in range(count)])


def fetch_y(value, step):
    return fetch(value, "seq", lambda i: i // Y * Y + (i + step) % Y)


def gathered(value, axis):
    size = lax.axis_size(axis)
    many = jnp.broadcast_to(value[None], (size,) + value.shape)
    return lax.all_to_all(many, axis, 0, 0, tiled=True)


Y_RING = [[z * Y + y for y in range(Y)] for z in range(Z)]
Z_RING = [[z * Y + y for z in range(Z)] for y in range(Y)]


def joined(value, groups):
    return lax.all_gather(value, "seq", axis_index_groups=groups, axis=0, tiled=True)


def local(queries, keys, values, head_temp, norm_gain):
    seq_size = lax.axis_size("seq")
    dev = lax.axis_index("seq").astype(jnp.int32).reshape(1)
    temp = head_temp * F32(math.log2(math.e) / math.sqrt(HEAD_DIM))
    up, down, one, two, three = prep(keys, values)

    group_two = joined(two, Y_RING)
    up, down, three, group_two = lax.optimization_barrier((up, down, three, group_two))
    from_up = fetch(up, "seq", lambda i: i - 1)
    from_down = fetch(down, "seq", lambda i: i + 1)
    low_side = dev[0] % Y < 2
    other_half = jnp.where(low_side, group_two[128:], group_two[:128])
    beyond = fetch(other_half, "seq", lambda i: i - Y if i % Y < 2 else i + Y)

    column = joined(three, Z_RING)
    column, from_up, from_down, beyond = lax.optimization_barrier(
        (column, from_up, from_down, beyond)
    )
    near_args = (queries, keys, values, from_up, from_down, one, group_two, beyond)
    acc_a, ml_a = near(0, seq_size, dev, temp, *near_args)
    acc_b, ml_b = near(1, seq_size, dev, temp, *near_args)
    after = fetch_y(column, 1)
    before = fetch_y(column, -1)
    half_a, half_b, acc_a, ml_a, acc_b, ml_b = lax.optimization_barrier(
        (after[:, :512], before[:, 512:], acc_a, ml_a, acc_b, ml_b)
    )
    opposite_a = fetch_y(half_a, 1)
    opposite_b = fetch_y(half_b, -1)

    gain = norm_gain.reshape(1, 512)
    att_a, sum_a = far(0, dev, temp, queries, acc_a, ml_a, gain, (column, after, opposite_a, before), None)
    att_b, sums = far(1, dev, temp, queries, acc_b, ml_b, gain, (column, after, opposite_b, before), sum_a)
    sums = gathered(sums, "head").reshape(8, ROWS)
    return norm(att_a, att_b, sums)


def solution(mesh):
    return jax.shard_map(
        local,
        mesh=mesh,
        in_specs=(P("seq", "head"), P("seq", "head"), P("seq", "head"), P("head"), P("head")),
        out_specs=P("seq", "head"),
        check_vma=False,
    )
```
